512 devices in a mesh: orig: 32 (over z_lo, y), dest: 16 (over z_hi, x, core).
Axes of the slice: x: 4, y: 8, z: 8 (z_hi: 2, z_lo: 4; z = z_hi * 4 + z_lo), core: 2. Of those that a mesh axis runs over, the one named last changes fastest.
Arguments:
- log_cost: bfloat16 [16384, 16384], P('orig', 'dest'), may hold values from 0 to 0.59765625
- elasticity: float32 [8], replicated, may hold values from 3 to 9
- productivity: float32 [8, 16384], P(None, 'orig'), may hold values from 0.3 to 3
- preference: float32 [8, 16384], P(None, 'dest'), may hold values from 0.2 to 5
- workers: float32 [16384], P('orig'), may hold values from 1 to 30
- start_wage: float32 [16384], P('orig'), may hold values from 0.2 to 5
Outputs:
- wage: float32 [16384], P('orig')
- log_price: float32 [8, 16384], P(None, 'dest')
The draws below stay inside these ranges and needn't reach their ends.
All inputs are finite; a program needn't handle non-finite values.
Results may differ from the reference program's by a relative error of at most 0.0003.
Values sent between devices are 32-bit elements; how exact they have to be, the bound alone decides.
No kernel may reach another device: no remote copies, remote signals or barrier semaphores. Data moves between devices by JAX's collectives and lax.ppermute only.
A program may use at most 64 MiB of HBM per device.

```python
import math
import jax
import jax.numpy as jnp
from jax import lax

SECTORS = 8
ITERS = 3
CELLS = 16384


def draw_workers(key, part):
    key = jax.random.fold_in(key, 11)
    ramp = 1.0 + 2.0 * jnp.arange(CELLS, dtype=jnp.float32) / float(max(CELLS - 1, 1))
    base = jnp.exp(jax.random.uniform(key, (CELLS,), jnp.float32, 0.0, math.log(10.0)))
    return base * ramp


def block_scale(key, extent, pieces, low, largest):
    level, own = 1.0, jax.random.fold_in(key, 6)
    for dim, blocks in pieces:
        heights = jnp.exp(jax.random.uniform(jax.random.fold_in(own, dim), (blocks,), jnp.float32, low / len(pieces), largest / len(pieces)))
        level = level * jnp.repeat(heights, extent[dim] // blocks).reshape([-1 if axis == dim else 1 for axis in range(len(extent))])
    return level


def setup_inputs(seed: int = 0) -> dict:
    splits = jax.random.split(jax.random.key(seed), 7)
    return {
        "log_cost": jnp.clip(0.59765625 * jax.random.uniform(splits[0], (CELLS, CELLS), jnp.float32) ** block_scale(splits[0], (CELLS, CELLS), ((0, 32), (1, 16)), -0.2, 0.2), 0.0, 0.59765625).astype(jnp.bfloat16),
        "elasticity": jnp.clip(jnp.exp(jax.random.uniform(splits[1], (SECTORS,), jnp.float32, math.log(3.0), math.log(9.0))), 3.0, 9.0),
        "productivity": jnp.clip(jnp.exp(math.log(3.0) - 2.3025851 * jax.random.uniform(splits[2], (SECTORS, CELLS), jnp.float32) ** block_scale(splits[2], (SECTORS, CELLS), ((1, 32),), -0.2, 0.2)), 0.3, 3.0),
        "preference": jnp.clip(jnp.exp(math.log(5.0) - 3.218876 * jax.random.uniform(splits[3], (SECTORS, CELLS), jnp.float32) ** block_scale(splits[3], (SECTORS, CELLS), ((1, 16),), -0.2, 0.2)), 0.2, 5.0),
        "workers": draw_workers(jax.random.fold_in(splits[6], 71), 0),
        "start_wage": jnp.clip(jnp.exp(math.log(5.0) - 3.218876 * jax.random.uniform(splits[5], (CELLS,), jnp.float32) ** block_scale(splits[5], (CELLS,), ((0, 32),), -0.2, 0.2)), 0.2, 5.0),
    }


def price_sums(log_cost, slope, supply_row):
    block_rows = min(1024, CELLS)
    blocks = log_cost.reshape(CELLS // block_rows, block_rows, CELLS)
    weights = supply_row.reshape(CELLS // block_rows, block_rows)

    def add_block(carry, pair):
        kernel = jnp.exp(-slope * pair[0].astype(jnp.float32))
        return (carry + jnp.dot(pair[1], kernel, precision=lax.Precision.HIGHEST), None)
    summed, _ = lax.scan(add_block, jnp.zeros((CELLS,), jnp.float32), (blocks, weights))
    return summed

def sales_terms(log_cost, slope, ratio_row):
    block_rows = min(1024, CELLS)
    blocks = log_cost.reshape(CELLS // block_rows, block_rows, CELLS)

    def one_block(block):
        kernel = jnp.exp(-slope * block.astype(jnp.float32))
        return jnp.dot(kernel, ratio_row, precision=lax.Precision.HIGHEST)
    return lax.map(one_block, blocks).reshape(CELLS)

def reference(log_cost, elasticity, productivity, preference, workers, start_wage):
    spend_share = preference / lax.optimization_barrier(jnp.sum(preference, axis=0, keepdims=True))
    wage = start_wage * (CELLS / jnp.sum(start_wage * workers))
    for step in range(ITERS):
        supply = productivity * jnp.exp(-elasticity[:, None] * jnp.log(wage)[None, :])
        spending = spend_share * (wage * workers)[None, :]
        phi = jnp.stack([price_sums(log_cost, elasticity[sector], supply[sector]) for sector in range(SECTORS)])
        ratio = spending / phi
        revenue = jnp.zeros_like(wage)
        for sector in range(SECTORS):
            revenue = revenue + supply[sector] * sales_terms(log_cost, elasticity[sector], ratio[sector])
        raw_wage = wage * jnp.sqrt(revenue / (wage * workers))
        wage = raw_wage * (CELLS / jnp.sum(raw_wage * workers))
    log_price = -jnp.log(phi) / elasticity[:, None]
    return (wage, log_price)
```

```python
import functools

import jax
import jax.numpy as jnp
from jax import lax
from jax.experimental import pallas as pl
from jax.experimental.pallas import tpu as pltpu
from jax.sharding import PartitionSpec as P

ITERS = 3
LANES = 128
LOG2E = 1.4426950408889634
CENTRE = 2048.0
SMALLEST, LARGEST = 1e-36, 1e30


def f32(*shape):
    return jax.ShapeDtypeStruct(shape, jnp.float32)


def pick(vector_ref, count):
    row = lax.broadcasted_iota(jnp.int32, (count, LANES), 0)
    out = jnp.zeros((count, LANES), jnp.float32)
    for j in range(count):
        out = jnp.where(row == j, vector_ref[j], out)
    return out


def total_of(x):
    return jnp.sum(jnp.sum(x, axis=0, keepdims=True), axis=1, keepdims=True)


def next_wage(wage_ref, workers_ref, sales_ref):
    wage, workers = wage_ref[...], workers_ref[...]
    revenue = jnp.sum(sales_ref[...], axis=0)
    return wage * jnp.sqrt(revenue / (wage * workers))


def supply_of(slopes, productivity_ref, wage):
    log_wage = jnp.log(wage)
    pieces = wage.shape[0]
    return [
        productivity_ref[:, p * LANES:(p + 1) * LANES] * jnp.exp(-slopes * log_wage[p:p + 1])
        for p in range(pieces)
    ]


def prepare(place_ref, slope_ref, productivity_ref, workers_ref, wage, send_ref, spread_ref):
    sectors, rows = productivity_ref.shape
    pieces = rows // LANES
    own = send_ref.shape[1] - 2
    owners = sectors // own
    blocks = send_ref.shape[0] // owners
    supply = supply_of(pick(slope_ref, sectors), productivity_ref, wage)
    for p in range(pieces):
        column = jnp.transpose(supply[p])
        for r in range(0, LANES, 8):
            for j in range(sectors):
                spread_ref[j, p * LANES + r:p * LANES + r + 8, :] = jnp.broadcast_to(column[r:r + 8, j:j + 1], (8, LANES))
    least = functools.reduce(jnp.minimum, supply)
    least = jnp.min(jnp.min(least, axis=0, keepdims=True), axis=1, keepdims=True)
    income = wage * workers_ref[...]
    world = jnp.where(least > SMALLEST, jnp.sum(income, axis=0, keepdims=True), jnp.nan)
    for k in range(blocks):
        piece = income[k % pieces:k % pieces + 1] * place_ref[k // pieces]
        for q in range(owners):
            send_ref[k * owners + q, own:own + 1, :] = piece
            send_ref[k * owners + q, own + 1:own + 2, :] = world


def send_phi(totals_ref, send_ref):
    sectors = totals_ref.shape[0]
    own = send_ref.shape[1] - 2
    owners = sectors // own
    for j in range(sectors):
        for k in range(send_ref.shape[0] // owners):
            piece = jnp.sum(totals_ref[j, :, k * LANES:(k + 1) * LANES], axis=0, keepdims=True)
            send_ref[k * owners + j // own, j % own:j % own + 1, :] = piece


def first_phi_kernel(place_ref, slope_ref, cost_ref, productivity_ref, workers_ref, wage_ref, send_ref, spread_ref, trade_ref, totals_ref):
    sectors, rows = productivity_ref.shape
    columns = cost_ref.shape[1]
    prepare(place_ref, slope_ref, productivity_ref, workers_ref, wage_ref[...], send_ref, spread_ref)
    scale = [slope_ref[j] * -LOG2E for j in range(sectors)]
    width = 2
    for first in range(0, columns // LANES, width):
        at_lanes = [slice((first + k) * LANES, (first + k + 1) * LANES) for k in range(width)]

        def step(block, totals):
            totals = list(totals)
            at = pl.ds(pl.multiple_of(block * 16, 16), 16)
            for k in range(width):
                cost = cost_ref[at, at_lanes[k]].astype(jnp.float32)
                for j in range(sectors):
                    trade = jnp.exp2(cost * scale[j])
                    trade_ref[j, at, at_lanes[k]] = trade
                    term = trade * spread_ref[j, at, :]
                    totals[j * width + k] += term[:8] + term[8:]
            return tuple(totals)

        zero = jnp.zeros((8, LANES), jnp.float32)
        totals = lax.fori_loop(0, rows // 16, step, (zero,) * (sectors * width), unroll=2)
        for j in range(sectors):
            for k in range(width):
                totals_ref[j, :, at_lanes[k]] = totals[j * width + k]
    send_phi(totals_ref, send_ref)


def phi_kernel(place_ref, slope_ref, trade_ref, productivity_ref, workers_ref, wage_ref, sales_ref, send_ref, spread_ref, new_wage_ref, totals_ref):
    sectors, rows, columns = trade_ref.shape
    blocks = columns // LANES
    wage = next_wage(wage_ref, workers_ref, sales_ref)
    new_wage_ref[...] = wage
    prepare(place_ref, slope_ref, productivity_ref, workers_ref, wage, send_ref, spread_ref)
    for j in range(sectors):
        def step(block, totals):
            at = pl.ds(pl.multiple_of(block * 8, 8), 8)
            weight = spread_ref[j, at, :]
            return tuple(totals[k] + trade_ref[j, at, k * LANES:(k + 1) * LANES] * weight for k in range(blocks))

        zero = jnp.zeros((8, LANES), jnp.float32)
        totals = lax.fori_loop(0, rows // 8, step, (zero,) * blocks, unroll=16)
        for k in range(blocks):
            totals_ref[j, :, k * LANES:(k + 1) * LANES] = totals[k]
    send_phi(totals_ref, send_ref)


def ratio_kernel(last, cells, place_ref, slope_ref, preference_ref, got_ref, send_ref):
    sectors = preference_ref.shape[0]
    own = got_ref.shape[1] - 2
    got = jnp.sum(got_ref[...], axis=0)
    income = got[own:own + 1]
    world = jnp.sum(got[own + 1:own + 2], axis=1, keepdims=True)
    factor = cells / world
    at = pl.multiple_of(place_ref[0] * LANES, LANES)
    preference = preference_ref[:, pl.ds(at, LANES)]
    spend_all = jnp.sum(preference, axis=0, keepdims=True)
    row = lax.broadcasted_iota(jnp.int32, (sectors, LANES), 0)
    centred = factor * CENTRE
    for s in range(own):
        sector = place_ref[1] * own + s
        wanted = jnp.sum(jnp.where(row == sector, preference, 0.0), axis=0, keepdims=True)
        phi = got[s:s + 1]
        ratio = wanted / spend_all * income / phi
        ratio = jnp.where(phi < LARGEST, ratio * (centred * centred), jnp.nan)
        send_ref[:, s, :] = jnp.broadcast_to(ratio, (send_ref.shape[0], LANES))
        if last:
            price = jnp.log(factor) - jnp.log(phi) / slope_ref[sector]
            send_ref[:, own + s, :] = jnp.broadcast_to(price, (send_ref.shape[0], LANES))


def sales_kernel(last, trade_ref, spread_ref, ratio_ref, send_ref, *rest):
    total_ref = rest[-1]
    sectors, rows, columns = trade_ref.shape
    blocks = columns // LANES
    owners = ratio_ref.shape[0] // blocks
    own = sectors // owners
    if last:
        price_ref = rest[0]
        for k in range(blocks):
            for j in range(sectors):
                price_ref[j:j + 1, k * LANES:(k + 1) * LANES] = ratio_ref[k * owners + j // own, own + j % own:own + j % own + 1, :]
    for j in range(sectors):
        ratios = [
            jnp.broadcast_to(ratio_ref[k * owners + j // own, j % own:j % own + 1, :], (8, LANES))
            for k in range(blocks)
        ]

        def step(block, carry):
            at = pl.ds(pl.multiple_of(block * 8, 8), 8)
            terms = [trade_ref[j, at, k * LANES:(k + 1) * LANES] * ratios[k] for k in range(blocks)]
            while len(terms) > 1:
                terms = [a + b for a, b in zip(terms[::2], terms[1::2])]
            total = terms[0] * spread_ref[j, at, :]
            total_ref[at, :] = total if j == 0 else total_ref[at, :] + total
            return carry

        lax.fori_loop(0, rows // 8, step, 0, unroll=8)
    for p in range(rows // LANES):
        piece = jnp.sum(jnp.transpose(total_ref[p * LANES:(p + 1) * LANES, :]), axis=0, keepdims=True)
        send_ref[:, p, :] = jnp.broadcast_to(piece, (send_ref.shape[0], LANES))


def settle_kernel(workers_ref, wage_ref, sales_ref, raw_ref, send_ref):
    raw = next_wage(wage_ref, workers_ref, sales_ref)
    raw_ref[...] = raw
    world = jnp.sum(raw * workers_ref[...], axis=0, keepdims=True)
    send_ref[:, 0, :] = jnp.broadcast_to(world, (send_ref.shape[0], LANES))


def finish_kernel(cells, raw_ref, got_ref, wage_ref, world_ref):
    world = total_of(got_ref[:, 0, :])
    wage_ref[...] = raw_ref[...] * (cells / world)
    world_ref[...] = jnp.broadcast_to(world, (1, LANES))


VM = pl.BlockSpec(memory_space=pltpu.VMEM)
SM = pl.BlockSpec(memory_space=pltpu.SMEM)


def call(body, out_shape, scalars, arrays, scratch=()):
    return pl.pallas_call(
        body,
        out_shape=tuple(out_shape),
        in_specs=[SM] * len(scalars) + [VM] * len(arrays),
        out_specs=(VM,) * len(out_shape),
        scratch_shapes=[pltpu.VMEM(shape, jnp.float32) for shape in scratch],
        compiler_params=pltpu.CompilerParams(vmem_limit_bytes=16 << 20),
    )(*scalars, *arrays)


def exchange(x, axis):
    return lax.all_to_all(x, axis, 0, 0, tiled=True)


def careful(log_cost, elasticity, productivity, preference, workers, start_wage):
    rows = log_cost.shape[0]
    columns = log_cost.shape[1]
    cells = rows * lax.axis_size("orig")
    spend_share = preference / jnp.sum(preference, axis=0, keepdims=True)

    def settle(raw_wage, wanted):
        local_income = None
        world_income = lax.psum(jnp.sum(raw_wage * workers), "orig")
        factor = cells / world_income
        wage = raw_wage * factor
        if wanted:
            incomes = lax.all_gather(wage * workers, "orig", axis=0, tiled=True)
            local_income = lax.dynamic_slice_in_dim(
                incomes, lax.axis_index("dest") * columns, columns
            )
        return (wage, local_income)

    def kernel_of(slope):
        return jnp.exp(-slope * log_cost.astype(jnp.float32))

    def phi_term(pair):
        return jnp.dot(pair[1], kernel_of(pair[0]), precision=lax.Precision.HIGHEST)

    def sales_term(pair):
        return jnp.dot(kernel_of(pair[0]), pair[1], precision=lax.Precision.HIGHEST)

    wage, dest_income = settle(start_wage, True)
    for step in range(ITERS):
        supply = productivity * jnp.exp(-elasticity[:, None] * jnp.log(wage)[None, :])
        spending = spend_share * dest_income[None, :]
        partial_phi = lax.map(phi_term, (elasticity, supply))
        price_part = lax.psum_scatter(partial_phi, "orig", scatter_dimension=1, tiled=True)
        part_width = price_part.shape[1]
        own_spending = lax.dynamic_slice_in_dim(
            spending, lax.axis_index("orig") * part_width, part_width, 1
        )
        ratio, log_price = (
            lax.all_gather(own_spending / price_part, "orig", axis=1, tiled=True),
            lax.all_gather(-jnp.log(price_part) / elasticity[:, None], "orig", axis=1, tiled=True),
        )
        partial_sales = lax.map(sales_term, (elasticity, ratio))
        sector_sales = lax.psum(partial_sales, "dest")
        revenue = jnp.sum(supply * sector_sales, axis=0)
        raw_wage = wage * jnp.sqrt(revenue / (wage * workers))
        wage, dest_income = settle(raw_wage, step + 1 < ITERS)
    return (wage, log_price)


def fast(log_cost, elasticity, productivity, preference, workers, start_wage):
    sectors, rows = productivity.shape
    columns = log_cost.shape[1]
    across, along = lax.axis_size("orig"), lax.axis_size("dest")
    cells = float(rows * across)
    blocks, pieces = columns // LANES, rows // LANES
    owners = across // blocks
    own = sectors // owners
    orig, dest = lax.axis_index("orig"), lax.axis_index("dest")
    part = orig - dest * (columns // rows)
    place = jnp.stack([orig // owners, orig % owners]).astype(jnp.int32)
    here = (part == jnp.arange(columns // rows)).astype(jnp.float32)
    workers = workers.reshape(pieces, LANES)
    wage = start_wage.reshape(pieces, LANES)
    sales = trade = None
    for step in range(ITERS):
        last = step + 1 == ITERS
        outs = [f32(across, own + 2, LANES), f32(sectors, rows, LANES)]
        scratch = [(sectors, 8, columns)]
        if step == 0:
            send, spread, trade = call(
                first_phi_kernel, outs + [f32(sectors, rows, columns)], [here, elasticity],
                [log_cost, productivity, workers, wage], scratch,
            )
        else:
            send, spread, wage = call(
                phi_kernel, outs + [f32(pieces, LANES)], [here, elasticity],
                [trade, productivity, workers, wage, sales], scratch,
            )
        got = exchange(send, "orig")
        ratio, = call(
            functools.partial(ratio_kernel, last, cells),
            [f32(across, 2 * own if last else own, LANES)],
            [place, elasticity],
            [preference, got],
        )
        ratio = exchange(ratio, "orig")
        made = call(
            functools.partial(sales_kernel, last),
            [f32(along, pieces, LANES)] + ([f32(sectors, columns)] if last else []),
            [],
            [trade, spread, ratio],
            [(rows, LANES)],
        )
        sales = exchange(made[0], "dest")
    log_price = made[1]
    raw, send = call(settle_kernel, [f32(pieces, LANES), f32(across, 1, LANES)], [], [workers, wage, sales])
    got = exchange(send, "orig")
    wage, world = call(functools.partial(finish_kernel, cells), [f32(pieces, LANES), f32(1, LANES)], [], [raw, got])
    return wage.reshape(rows), log_price, world[0, 0]


def on_device(*args):
    wage, log_price, world = fast(*args)
    return lax.cond(jnp.isfinite(world), lambda: (wage, log_price), lambda: careful(*args))


def solution(mesh):
    return jax.shard_map(
        on_device,
        mesh=mesh,
        in_specs=(P("orig", "dest"), P(), P(None, "orig"), P(None, "dest"), P("orig"), P("orig")),
        out_specs=(P("orig"), P(None, "dest")),
        check_vma=False,
    )
```

```python
import functools

import jax
import jax.numpy as jnp
from jax import lax
from jax.experimental import pallas as pl
from jax.experimental.pallas import tpu as pltpu
from jax.sharding import PartitionSpec as P

ITERS = 3
LANES = 128
CENTRE = 1024.0
SMALLEST, LARGEST = 1e-32, 1e30


def f32(*shape):
    return jax.ShapeDtypeStruct(shape, jnp.float32)


def tree_sum(terms):
    while len(terms) > 1:
        terms = [a + b for a, b in zip(terms[::2], terms[1::2])]
    return terms[0]


def pick(vector_ref, count):
    row = lax.broadcasted_iota(jnp.int32, (count, LANES), 0)
    out = jnp.zeros((count, LANES), jnp.float32)
    for j in range(count):
        out = jnp.where(row == j, vector_ref[j], out)
    return out


def total_of(x):
    return jnp.sum(jnp.sum(x, axis=0, keepdims=True), axis=1, keepdims=True)


def next_wage(wage_ref, workers_ref, sales_ref):
    wage, workers = wage_ref[...], workers_ref[...]
    revenue = jnp.sum(sales_ref[...], axis=0)
    return wage * jnp.sqrt(revenue / (wage * workers))


def supply_of(slopes, productivity_ref, wage):
    log_wage = jnp.log(wage)
    pieces = wage.shape[0]
    return [
        productivity_ref[:, p * LANES:(p + 1) * LANES] * jnp.exp(-slopes * log_wage[p:p + 1])
        for p in range(pieces)
    ]


def spread_over_lanes(supply_ref, spread_ref):
    sectors = supply_ref.shape[0]
    row = lax.broadcasted_iota(jnp.int32, (sectors, sectors * LANES), 0)
    lane = lax.broadcasted_iota(jnp.int32, (sectors, sectors * LANES), 1)
    ones = jnp.where((lane >= row * LANES) & (lane < (row + 1) * LANES), 1.0, 0.0).astype(jnp.bfloat16)
    rest, terms = supply_ref[...], []
    for _ in range(3):
        terms.append(rest.astype(jnp.bfloat16))
        rest = rest - terms[-1].astype(jnp.float32)
    spread_ref[...] = lax.dot_general(
        jnp.concatenate(terms, axis=0), jnp.concatenate([ones] * 3, axis=0), (((0,), (0,)), ((), ())),
        preferred_element_type=jnp.float32,
    )


def prepare(spot_ref, slope_ref, columns, productivity_ref, workers_ref, wage, send_ref, spread_ref, supply_ref):
    sectors, rows = productivity_ref.shape
    pieces = rows // LANES
    own = send_ref.shape[1] - 2
    owners = sectors // own
    blocks = send_ref.shape[0] // owners
    supply = supply_of(pick(slope_ref, sectors), productivity_ref, wage)
    for p in range(pieces):
        supply_ref[:, p * LANES:(p + 1) * LANES] = supply[p]
    spread_over_lanes(supply_ref, spread_ref)
    least = functools.reduce(jnp.minimum, supply)
    least = jnp.min(jnp.min(least, axis=0, keepdims=True), axis=1, keepdims=True)
    income = wage * workers_ref[...]
    world = jnp.where(least > SMALLEST, jnp.sum(income, axis=0, keepdims=True), jnp.nan)
    part = spot_ref[0] - spot_ref[1] * (columns // rows)
    for i in range(columns // rows):
        here = income * jnp.where(part == i, 1.0, 0.0)
        for p in range(pieces):
            for q in range(owners):
                at = (i * pieces + p) * owners + q
                send_ref[at, own:own + 1, :] = here[p:p + 1]
                send_ref[at, own + 1:own + 2, :] = world


def send_phi(totals_ref, send_ref):
    sectors = totals_ref.shape[0]
    own = send_ref.shape[1] - 2
    owners = sectors // own
    for j in range(sectors):
        for k in range(send_ref.shape[0] // owners):
            piece = jnp.sum(totals_ref[j, :, k * LANES:(k + 1) * LANES], axis=0, keepdims=True)
            send_ref[k * owners + j // own, j % own:j % own + 1, :] = piece


def first_phi_kernel(spot_ref, slope_ref, cost_ref, productivity_ref, workers_ref, wage_ref, send_ref, spread_ref, trade_ref, totals_ref, supply_ref):
    sectors, rows = productivity_ref.shape
    columns = cost_ref.shape[1]
    prepare(spot_ref, slope_ref, columns, productivity_ref, workers_ref, wage_ref[...], send_ref, spread_ref, supply_ref)
    slopes = [-slope_ref[j] for j in range(sectors)]
    totals_ref[...] = jnp.zeros_like(totals_ref)
    height = 32

    def step(block, carry):
        at = pl.ds(pl.multiple_of(block * height, height), height)
        for k in range(columns // LANES):
            lanes = slice(k * LANES, (k + 1) * LANES)
            cost = cost_ref[at, lanes].astype(jnp.float32)
            for j in range(sectors):
                trade = jnp.exp(cost * slopes[j])
                trade_ref[j, at, lanes] = trade
                term = trade * spread_ref[at, j * LANES:(j + 1) * LANES]
                totals_ref[j, :, lanes] += tree_sum([term[r:r + 8] for r in range(0, height, 8)])
        return carry

    lax.fori_loop(0, rows // height, step, 0)
    send_phi(totals_ref, send_ref)


def phi_kernel(spot_ref, slope_ref, trade_ref, productivity_ref, workers_ref, wage_ref, sales_ref, send_ref, spread_ref, new_wage_ref, totals_ref, supply_ref):
    sectors, rows, columns = trade_ref.shape
    blocks = columns // LANES
    wage = next_wage(wage_ref, workers_ref, sales_ref)
    new_wage_ref[...] = wage
    prepare(spot_ref, slope_ref, columns, productivity_ref, workers_ref, wage, send_ref, spread_ref, supply_ref)
    for j in range(sectors):
        def step(block, totals):
            at = pl.ds(pl.multiple_of(block * 8, 8), 8)
            weight = spread_ref[at, j * LANES:(j + 1) * LANES]
            return tuple(totals[k] + trade_ref[j, at, k * LANES:(k + 1) * LANES] * weight for k in range(blocks))

        zero = jnp.zeros((8, LANES), jnp.float32)
        totals = lax.fori_loop(0, rows // 8, step, (zero,) * blocks, unroll=16)
        for k in range(blocks):
            totals_ref[j, :, k * LANES:(k + 1) * LANES] = totals[k]
    send_phi(totals_ref, send_ref)


def ratio_kernel(last, cells, spot_ref, slope_ref, preference_ref, got_ref, send_ref):
    sectors = preference_ref.shape[0]
    own = got_ref.shape[1] - 2
    got = jnp.sum(got_ref[...], axis=0)
    income = got[own:own + 1]
    world = jnp.sum(got[own + 1:own + 2], axis=1, keepdims=True)
    factor = cells / world
    owners = sectors // own
    at = pl.multiple_of(lax.div(spot_ref[0], owners) * LANES, LANES)
    preference = preference_ref[:, pl.ds(at, LANES)]
    spend_all = jnp.sum(preference, axis=0, keepdims=True)
    row = lax.broadcasted_iota(jnp.int32, (sectors, LANES), 0)
    centred = factor * CENTRE
    for s in range(own):
        sector = lax.rem(spot_ref[0], owners) * own + s
        wanted = jnp.sum(jnp.where(row == sector, preference, 0.0), axis=0, keepdims=True)
        phi = got[s:s + 1]
        ratio = wanted / spend_all * income / phi
        ratio = jnp.where(phi < LARGEST, ratio * (centred * centred), jnp.nan)
        send_ref[:, s, :] = jnp.broadcast_to(ratio, (send_ref.shape[0], LANES))
        if last:
            price = jnp.log(factor) - jnp.log(phi) / slope_ref[sector]
            send_ref[:, own + s, :] = jnp.broadcast_to(price, (send_ref.shape[0], LANES))


def sales_kernel(last, trade_ref, spread_ref, ratio_ref, send_ref, *rest):
    total_ref = rest[-1]
    sectors, rows, columns = trade_ref.shape
    blocks = columns // LANES
    owners = ratio_ref.shape[0] // blocks
    own = sectors // owners
    if last:
        price_ref = rest[0]
        for k in range(blocks):
            for j in range(sectors):
                price_ref[j:j + 1, k * LANES:(k + 1) * LANES] = ratio_ref[k * owners + j // own, own + j % own:own + j % own + 1, :]
    for j in range(sectors):
        ratios = [
            jnp.broadcast_to(ratio_ref[k * owners + j // own, j % own:j % own + 1, :], (8, LANES))
            for k in range(blocks)
        ]

        def step(block, carry):
            at = pl.ds(pl.multiple_of(block * 8, 8), 8)
            terms = [trade_ref[j, at, k * LANES:(k + 1) * LANES] * ratios[k] for k in range(blocks)]
            total = tree_sum(terms) * spread_ref[at, j * LANES:(j + 1) * LANES]
            total_ref[at, :] = total if j == 0 else total_ref[at, :] + total
            return carry

        lax.fori_loop(0, rows // 8, step, 0, unroll=8)
    for p in range(rows // LANES):
        piece = jnp.sum(jnp.transpose(total_ref[p * LANES:(p + 1) * LANES, :]), axis=0, keepdims=True)
        send_ref[:, p, :] = jnp.broadcast_to(piece, (send_ref.shape[0], LANES))


def settle_kernel(workers_ref, wage_ref, sales_ref, raw_ref, send_ref):
    raw = next_wage(wage_ref, workers_ref, sales_ref)
    raw_ref[...] = raw
    world = jnp.sum(raw * workers_ref[...], axis=0, keepdims=True)
    send_ref[:, 0, :] = jnp.broadcast_to(world, (send_ref.shape[0], LANES))


def finish_kernel(cells, raw_ref, got_ref, wage_ref, world_ref):
    world = total_of(got_ref[:, 0, :])
    wage_ref[...] = raw_ref[...] * (cells / world)
    world_ref[...] = jnp.broadcast_to(world, (1, LANES))


VM = pl.BlockSpec(memory_space=pltpu.VMEM)
SM = pl.BlockSpec(memory_space=pltpu.SMEM)


def call(body, out_shape, scalars, arrays, scratch=()):
    return pl.pallas_call(
        body,
        out_shape=tuple(out_shape),
        in_specs=[SM] * len(scalars) + [VM] * len(arrays),
        out_specs=(VM,) * len(out_shape),
        scratch_shapes=[pltpu.VMEM(shape, jnp.float32) for shape in scratch],
        compiler_params=pltpu.CompilerParams(vmem_limit_bytes=16 << 20),
    )(*scalars, *arrays)


def exchange(x, axis):
    return lax.all_to_all(x, axis, 0, 0, tiled=True)


def careful(log_cost, elasticity, productivity, preference, workers, start_wage):
    rows = log_cost.shape[0]
    columns = log_cost.shape[1]
    cells = rows * lax.axis_size("orig")
    spend_share = preference / jnp.sum(preference, axis=0, keepdims=True)

    def settle(raw_wage, wanted):
        local_income = None
        world_income = lax.psum(jnp.sum(raw_wage * workers), "orig")
        factor = cells / world_income
        wage = raw_wage * factor
        if wanted:
            incomes = lax.all_gather(wage * workers, "orig", axis=0, tiled=True)
            local_income = lax.dynamic_slice_in_dim(
                incomes, lax.axis_index("dest") * columns, columns
            )
        return (wage, local_income)

    def kernel_of(slope):
        return jnp.exp(-slope * log_cost.astype(jnp.float32))

    def phi_term(pair):
        return jnp.dot(pair[1], kernel_of(pair[0]), precision=lax.Precision.HIGHEST)

    def sales_term(pair):
        return jnp.dot(kernel_of(pair[0]), pair[1], precision=lax.Precision.HIGHEST)

    wage, dest_income = settle(start_wage, True)
    for step in range(ITERS):
        supply = productivity * jnp.exp(-elasticity[:, None] * jnp.log(wage)[None, :])
        spending = spend_share * dest_income[None, :]
        partial_phi = lax.map(phi_term, (elasticity, supply))
        price_part = lax.psum_scatter(partial_phi, "orig", scatter_dimension=1, tiled=True)
        part_width = price_part.shape[1]
        own_spending = lax.dynamic_slice_in_dim(
            spending, lax.axis_index("orig") * part_width, part_width, 1
        )
        ratio, log_price = (
            lax.all_gather(own_spending / price_part, "orig", axis=1, tiled=True),
            lax.all_gather(-jnp.log(price_part) / elasticity[:, None], "orig", axis=1, tiled=True),
        )
        partial_sales = lax.map(sales_term, (elasticity, ratio))
        sector_sales = lax.psum(partial_sales, "dest")
        revenue = jnp.sum(supply * sector_sales, axis=0)
        raw_wage = wage * jnp.sqrt(revenue / (wage * workers))
        wage, dest_income = settle(raw_wage, step + 1 < ITERS)
    return (wage, log_price)


def fast(log_cost, elasticity, productivity, preference, workers, start_wage):
    sectors, rows = productivity.shape
    columns = log_cost.shape[1]
    across, along = lax.axis_size("orig"), lax.axis_size("dest")
    cells = float(rows * across)
    blocks, pieces = columns // LANES, rows // LANES
    own = sectors * blocks // across
    spot = jnp.stack([lax.axis_index("orig"), lax.axis_index("dest")]).astype(jnp.int32)
    workers = workers.reshape(pieces, LANES)
    wage = start_wage.reshape(pieces, LANES)
    sales = trade = None
    for step in range(ITERS):
        last = step + 1 == ITERS
        outs = [f32(across, own + 2, LANES), f32(rows, sectors * LANES)]
        scratch = [(sectors, 8, columns), (sectors, rows)]
        if step == 0:
            send, spread, trade = call(
                first_phi_kernel, outs + [f32(sectors, rows, columns)], [spot, elasticity],
                [log_cost, productivity, workers, wage], scratch,
            )
        else:
            send, spread, wage = call(
                phi_kernel, outs + [f32(pieces, LANES)], [spot, elasticity],
                [trade, productivity, workers, wage, sales], scratch,
            )
        got = exchange(send, "orig")
        ratio, = call(
            functools.partial(ratio_kernel, last, cells),
            [f32(across, 2 * own if last else own, LANES)],
            [spot, elasticity],
            [preference, got],
        )
        ratio = exchange(ratio, "orig")
        made = call(
            functools.partial(sales_kernel, last),
            [f32(along, pieces, LANES)] + ([f32(sectors, columns)] if last else []),
            [],
            [trade, spread, ratio],
            [(rows, LANES)],
        )
        sales = exchange(made[0], "dest")
    log_price = made[1]
    raw, send = call(settle_kernel, [f32(pieces, LANES), f32(across, 1, LANES)], [], [workers, wage, sales])
    got = exchange(send, "orig")
    wage, world = call(functools.partial(finish_kernel, cells), [f32(pieces, LANES), f32(1, LANES)], [], [raw, got])
    return wage.reshape(rows), log_price, world[0, 0]


def on_device(*args):
    wage, log_price, world = fast(*args)
    return lax.cond(jnp.isfinite(world), lambda: (wage, log_price), lambda: careful(*args))


def solution(mesh):
    return jax.shard_map(
        on_device,
        mesh=mesh,
        in_specs=(P("orig", "dest"), P(), P(None, "orig"), P(None, "dest"), P("orig"), P("orig")),
        out_specs=(P("orig"), P(None, "dest")),
        check_vma=False,
    )
```

```python
import functools

import jax
import jax.numpy as jnp
from jax import lax
from jax.experimental import pallas as pl
from jax.experimental.pallas import tpu as pltpu
from jax.sharding import PartitionSpec as P

ITERS = 3
LANES = 128
CENTRE = 1024.0
INNER = 8
SMALLEST, LARGEST = 1e-32, 1e30


def f32(*shape):
    return jax.ShapeDtypeStruct(shape, jnp.float32)


def tree_sum(terms):
    while len(terms) > 1:
        terms = [a + b for a, b in zip(terms[::2], terms[1::2])]
    return terms[0]


def pick(vector_ref, count):
    row = lax.broadcasted_iota(jnp.int32, (count, LANES), 0)
    out = jnp.zeros((count, LANES), jnp.float32)
    for j in range(count):
        out = jnp.where(row == j, vector_ref[j], out)
    return out


def total_of(x):
    return jnp.sum(jnp.sum(x, axis=0, keepdims=True), axis=1, keepdims=True)


def next_wage(wage_ref, workers_ref, sales_ref):
    wage, workers = wage_ref[...], workers_ref[...]
    revenue = jnp.sum(sales_ref[...], axis=0)
    return wage * jnp.sqrt(revenue / (wage * workers))


def supply_of(slopes, productivity_ref, wage):
    log_wage = jnp.log(wage)
    pieces = wage.shape[0]
    return [
        productivity_ref[:, p * LANES:(p + 1) * LANES] * jnp.exp(-slopes * log_wage[p:p + 1])
        for p in range(pieces)
    ]


def spread_over_lanes(supply_ref, spread_ref):
    sectors = supply_ref.shape[0]
    row = lax.broadcasted_iota(jnp.int32, (sectors, sectors * LANES), 0)
    lane = lax.broadcasted_iota(jnp.int32, (sectors, sectors * LANES), 1)
    ones = jnp.where((lane >= row * LANES) & (lane < (row + 1) * LANES), 1.0, 0.0).astype(jnp.bfloat16)
    rest, terms = supply_ref[...], []
    for _ in range(3):
        terms.append(rest.astype(jnp.bfloat16))
        rest = rest - terms[-1].astype(jnp.float32)
    spread_ref[...] = lax.dot_general(
        jnp.concatenate(terms, axis=0), jnp.concatenate([ones] * 3, axis=0), (((0,), (0,)), ((), ())),
        preferred_element_type=jnp.float32,
    )


def prepare(spot_ref, slope_ref, columns, productivity_ref, workers_ref, wage, part_ref, spread_ref, supply_ref):
    sectors, rows = productivity_ref.shape
    pieces = rows // LANES
    supply = supply_of(pick(slope_ref, sectors), productivity_ref, wage)
    for p in range(pieces):
        supply_ref[:, p * LANES:(p + 1) * LANES] = supply[p]
    spread_over_lanes(supply_ref, spread_ref)
    least = functools.reduce(jnp.minimum, supply)
    least = jnp.min(jnp.min(least, axis=0, keepdims=True), axis=1, keepdims=True)
    income = wage * workers_ref[...]
    part_ref[:, columns + LANES:] = jnp.zeros((sectors, LANES), jnp.float32)
    part_ref[:pieces, columns + LANES:] = jnp.where(least > SMALLEST, income, jnp.nan)
    part = spot_ref[0] - spot_ref[1] * (columns // rows)
    for i in range(columns // rows):
        here = jnp.where(part == i, 1.0, 0.0)
        part_ref[i * pieces:(i + 1) * pieces, columns:columns + LANES] = income * here


def send_phi(totals_ref, part_ref, send_ref):
    sectors, _, columns = totals_ref.shape
    for j in range(sectors):
        for k in range(columns // LANES):
            lanes = slice(k * LANES, (k + 1) * LANES)
            part_ref[j:j + 1, lanes] = jnp.sum(totals_ref[j, :, lanes], axis=0, keepdims=True)
    part = part_ref[...]
    for copy in range(send_ref.shape[0]):
        send_ref[copy] = part


def first_phi_kernel(spot_ref, slope_ref, cost_ref, productivity_ref, workers_ref, wage_ref, send_ref, spread_ref, trade_ref, totals_ref, supply_ref, part_ref):
    sectors, rows = productivity_ref.shape
    columns = cost_ref.shape[1]
    prepare(spot_ref, slope_ref, columns, productivity_ref, workers_ref, wage_ref[...], part_ref, spread_ref, supply_ref)
    slopes = [-slope_ref[j] for j in range(sectors)]
    totals_ref[...] = jnp.zeros_like(totals_ref)
    height = 32

    def step(block, carry):
        at = pl.ds(pl.multiple_of(block * height, height), height)
        for k in range(columns // LANES):
            lanes = slice(k * LANES, (k + 1) * LANES)
            cost = cost_ref[at, lanes].astype(jnp.float32)
            for j in range(sectors):
                trade = jnp.exp(cost * slopes[j])
                trade_ref[j, at, lanes] = trade
                term = trade * spread_ref[at, j * LANES:(j + 1) * LANES]
                totals_ref[j, :, lanes] += tree_sum([term[r:r + 8] for r in range(0, height, 8)])
        return carry

    lax.fori_loop(0, rows // height, step, 0)
    send_phi(totals_ref, part_ref, send_ref)


def phi_kernel(spot_ref, slope_ref, trade_ref, productivity_ref, workers_ref, wage_ref, sales_ref, send_ref, spread_ref, new_wage_ref, totals_ref, supply_ref, part_ref):
    sectors, rows, columns = trade_ref.shape
    blocks = columns // LANES
    wage = next_wage(wage_ref, workers_ref, sales_ref)
    new_wage_ref[...] = wage
    prepare(spot_ref, slope_ref, columns, productivity_ref, workers_ref, wage, part_ref, spread_ref, supply_ref)
    for j in range(sectors):
        def step(block, totals):
            at = pl.ds(pl.multiple_of(block * 8, 8), 8)
            weight = spread_ref[at, j * LANES:(j + 1) * LANES]
            return tuple(totals[k] + trade_ref[j, at, k * LANES:(k + 1) * LANES] * weight for k in range(blocks))

        zero = jnp.zeros((8, LANES), jnp.float32)
        totals = lax.fori_loop(0, rows // 8, step, (zero,) * blocks, unroll=16)
        for k in range(blocks):
            totals_ref[j, :, k * LANES:(k + 1) * LANES] = totals[k]
    send_phi(totals_ref, part_ref, send_ref)


def sum_kernel(got_ref, send_ref):
    total = jnp.sum(got_ref[...], axis=0)
    for copy in range(send_ref.shape[0]):
        send_ref[copy] = total


def sales_kernel(last, cells, slope_ref, trade_ref, spread_ref, preference_ref, got_ref, send_ref, *rest):
    total_ref, ratio_ref, sums_ref = rest[-3:]
    sectors, rows, columns = trade_ref.shape
    blocks = columns // LANES
    sums_ref[...] = jnp.sum(got_ref[...], axis=0)
    factor = cells / total_of(sums_ref[:, columns + LANES:])
    centred = (factor * CENTRE) * (factor * CENTRE)
    preference = preference_ref[...]
    share = preference / jnp.sum(preference, axis=0, keepdims=True)
    for k in range(blocks):
        lanes = slice(k * LANES, (k + 1) * LANES)
        phi = sums_ref[:, lanes]
        ratio = share[:, lanes] * sums_ref[k:k + 1, columns:columns + LANES] / phi
        ratio_ref[:, lanes] = jnp.where(phi < LARGEST, ratio * centred, jnp.nan)
    if last:
        slopes = pick(slope_ref, sectors)
        for k in range(blocks):
            lanes = slice(k * LANES, (k + 1) * LANES)
            rest[0][:, lanes] = jnp.log(factor) - jnp.log(sums_ref[:, lanes]) / slopes
    for j in range(sectors):
        ratios = [
            jnp.broadcast_to(ratio_ref[j:j + 1, k * LANES:(k + 1) * LANES], (8, LANES))
            for k in range(blocks)
        ]

        def step(block, carry):
            at = pl.ds(pl.multiple_of(block * 8, 8), 8)
            terms = [trade_ref[j, at, k * LANES:(k + 1) * LANES] * ratios[k] for k in range(blocks)]
            total = tree_sum(terms) * spread_ref[at, j * LANES:(j + 1) * LANES]
            total_ref[at, :] = total if j == 0 else total_ref[at, :] + total
            return carry

        lax.fori_loop(0, rows // 8, step, 0, unroll=8)
    for p in range(rows // LANES):
        piece = jnp.sum(jnp.transpose(total_ref[p * LANES:(p + 1) * LANES, :]), axis=0, keepdims=True)
        send_ref[:, p, :] = jnp.broadcast_to(piece, (send_ref.shape[0], LANES))


def settle_kernel(workers_ref, wage_ref, sales_ref, raw_ref, send_ref):
    raw = next_wage(wage_ref, workers_ref, sales_ref)
    raw_ref[...] = raw
    world = jnp.sum(raw * workers_ref[...], axis=0, keepdims=True)
    send_ref[:, 0, :] = jnp.broadcast_to(world, (send_ref.shape[0], LANES))


def finish_kernel(cells, raw_ref, got_ref, wage_ref, world_ref):
    world = total_of(got_ref[:, 0, :])
    wage_ref[...] = raw_ref[...] * (cells / world)
    world_ref[...] = jnp.broadcast_to(world, (1, LANES))


VM = pl.BlockSpec(memory_space=pltpu.VMEM)
SM = pl.BlockSpec(memory_space=pltpu.SMEM)


def call(body, out_shape, scalars, arrays, scratch=()):
    return pl.pallas_call(
        body,
        out_shape=tuple(out_shape),
        in_specs=[SM] * len(scalars) + [VM] * len(arrays),
        out_specs=(VM,) * len(out_shape),
        scratch_shapes=[pltpu.VMEM(shape, jnp.float32) for shape in scratch],
        compiler_params=pltpu.CompilerParams(vmem_limit_bytes=16 << 20),
    )(*scalars, *arrays)


def exchange(x, axis, groups=None):
    return lax.all_to_all(x, axis, 0, 0, tiled=True, axis_index_groups=groups)


def careful(log_cost, elasticity, productivity, preference, workers, start_wage):
    rows = log_cost.shape[0]
    columns = log_cost.shape[1]
    cells = rows * lax.axis_size("orig")
    spend_share = preference / jnp.sum(preference, axis=0, keepdims=True)

    def settle(raw_wage, wanted):
        local_income = None
        world_income = lax.psum(jnp.sum(raw_wage * workers), "orig")
        factor = cells / world_income
        wage = raw_wage * factor
        if wanted:
            incomes = lax.all_gather(wage * workers, "orig", axis=0, tiled=True)
            local_income = lax.dynamic_slice_in_dim(
                incomes, lax.axis_index("dest") * columns, columns
            )
        return (wage, local_income)

    def kernel_of(slope):
        return jnp.exp(-slope * log_cost.astype(jnp.float32))

    def phi_term(pair):
        return jnp.dot(pair[1], kernel_of(pair[0]), precision=lax.Precision.HIGHEST)

    def sales_term(pair):
        return jnp.dot(kernel_of(pair[0]), pair[1], precision=lax.Precision.HIGHEST)

    wage, dest_income = settle(start_wage, True)
    for step in range(ITERS):
        supply = productivity * jnp.exp(-elasticity[:, None] * jnp.log(wage)[None, :])
        spending = spend_share * dest_income[None, :]
        partial_phi = lax.map(phi_term, (elasticity, supply))
        price_part = lax.psum_scatter(partial_phi, "orig", scatter_dimension=1, tiled=True)
        part_width = price_part.shape[1]
        own_spending = lax.dynamic_slice_in_dim(
            spending, lax.axis_index("orig") * part_width, part_width, 1
        )
        ratio, log_price = (
            lax.all_gather(own_spending / price_part, "orig", axis=1, tiled=True),
            lax.all_gather(-jnp.log(price_part) / elasticity[:, None], "orig", axis=1, tiled=True),
        )
        partial_sales = lax.map(sales_term, (elasticity, ratio))
        sector_sales = lax.psum(partial_sales, "dest")
        revenue = jnp.sum(supply * sector_sales, axis=0)
        raw_wage = wage * jnp.sqrt(revenue / (wage * workers))
        wage, dest_income = settle(raw_wage, step + 1 < ITERS)
    return (wage, log_price)


def fast(log_cost, elasticity, productivity, preference, workers, start_wage):
    sectors, rows = productivity.shape
    columns = log_cost.shape[1]
    across, along = lax.axis_size("orig"), lax.axis_size("dest")
    cells = float(rows * across)
    pieces = rows // LANES
    outer = across // INNER
    by_inner = [[i * INNER + j for j in range(INNER)] for i in range(outer)]
    by_outer = [[i * INNER + j for i in range(outer)] for j in range(INNER)]
    width = columns + 2 * LANES
    spot = jnp.stack([lax.axis_index("orig"), lax.axis_index("dest")]).astype(jnp.int32)
    workers = workers.reshape(pieces, LANES)
    wage = start_wage.reshape(pieces, LANES)
    sales = trade = None
    for step in range(ITERS):
        last = step + 1 == ITERS
        outs = [f32(outer, sectors, width), f32(rows, sectors * LANES)]
        scratch = [(sectors, 8, columns), (sectors, rows), (sectors, width)]
        if step == 0:
            send, spread, trade = call(
                first_phi_kernel, outs + [f32(sectors, rows, columns)], [spot, elasticity],
                [log_cost, productivity, workers, wage], scratch,
            )
        else:
            send, spread, wage = call(
                phi_kernel, outs + [f32(pieces, LANES)], [spot, elasticity],
                [trade, productivity, workers, wage, sales], scratch,
            )
        got = exchange(send, "orig", by_outer)
        send, = call(sum_kernel, [f32(INNER, sectors, width)], [], [got])
        got = exchange(send, "orig", by_inner)
        made = call(
            functools.partial(sales_kernel, last, cells),
            [f32(along, pieces, LANES)] + ([f32(sectors, columns)] if last else []),
            [elasticity],
            [trade, spread, preference, got],
            [(rows, LANES), (sectors, columns), (sectors, width)],
        )
        sales = exchange(made[0], "dest")
    log_price = made[1]
    raw, send = call(settle_kernel, [f32(pieces, LANES), f32(across, 1, LANES)], [], [workers, wage, sales])
    got = exchange(send, "orig")
    wage, world = call(functools.partial(finish_kernel, cells), [f32(pieces, LANES), f32(1, LANES)], [], [raw, got])
    return wage.reshape(rows), log_price, world[0, 0]


def on_device(*args):
    wage, log_price, world = fast(*args)
    return lax.cond(jnp.isfinite(world), lambda: (wage, log_price), lambda: careful(*args))


def solution(mesh):
    return jax.shard_map(
        on_device,
        mesh=mesh,
        in_specs=(P("orig", "dest"), P(), P(None, "orig"), P(None, "dest"), P("orig"), P("orig")),
        out_specs=(P("orig"), P(None, "dest")),
        check_vma=False,
    )
```

```python
import functools

import jax
import jax.numpy as jnp
from jax import lax
from jax.experimental import pallas as pl
from jax.experimental.pallas import tpu as pltpu
from jax.sharding import PartitionSpec as P

ITERS = 3
LANES = 128
CENTRE = 1024.0
GAIN = 2.0
INNER = 8
SMALLEST, LARGEST = 1e-32, 1e30


def f32(*shape):
    return jax.ShapeDtypeStruct(shape, jnp.float32)


def tree_sum(terms):
    while len(terms) > 1:
        terms = [a + b for a, b in zip(terms[::2], terms[1::2])]
    return terms[0]


def pick(vector_ref, count):
    row = lax.broadcasted_iota(jnp.int32, (count, LANES), 0)
    out = jnp.zeros((count, LANES), jnp.float32)
    for j in range(count):
        out = jnp.where(row == j, vector_ref[j], out)
    return out


def total_of(x):
    return jnp.sum(jnp.sum(x, axis=0, keepdims=True), axis=1, keepdims=True)


def next_wage(wage_ref, workers_ref, sales_ref, gain=1.0):
    wage, workers = wage_ref[...], workers_ref[...]
    revenue = jnp.sum(sales_ref[...], axis=0)
    return wage * gain * jnp.sqrt(revenue / (wage * workers))


def supply_of(slopes, productivity_ref, wage):
    log_wage = jnp.log(wage)
    pieces = wage.shape[0]
    return [
        productivity_ref[:, p * LANES:(p + 1) * LANES] * jnp.exp(-slopes * log_wage[p:p + 1])
        for p in range(pieces)
    ]


def spread_over_lanes(supply_ref, spread_ref):
    sectors = supply_ref.shape[0]
    row = lax.broadcasted_iota(jnp.int32, (sectors, sectors * LANES), 0)
    lane = lax.broadcasted_iota(jnp.int32, (sectors, sectors * LANES), 1)
    ones = jnp.where((lane >= row * LANES) & (lane < (row + 1) * LANES), 1.0, 0.0).astype(jnp.bfloat16)
    rest, terms = supply_ref[...], []
    for _ in range(3):
        terms.append(rest.astype(jnp.bfloat16))
        rest = rest - terms[-1].astype(jnp.float32)
    spread_ref[...] = lax.dot_general(
        jnp.concatenate(terms, axis=0), jnp.concatenate([ones] * 3, axis=0), (((0,), (0,)), ((), ())),
        preferred_element_type=jnp.float32,
    )


def prepare(spot_ref, slope_ref, columns, productivity_ref, workers_ref, wage, part_ref, spread_ref, supply_ref):
    sectors, rows = productivity_ref.shape
    pieces = rows // LANES
    supply = supply_of(pick(slope_ref, sectors), productivity_ref, wage)
    for p in range(pieces):
        supply_ref[:, p * LANES:(p + 1) * LANES] = supply[p]
    spread_over_lanes(supply_ref, spread_ref)
    least = functools.reduce(jnp.minimum, supply)
    least = jnp.min(jnp.min(least, axis=0, keepdims=True), axis=1, keepdims=True)
    income = wage * workers_ref[...]
    guarded = jnp.where(least > SMALLEST, income, jnp.nan)
    part = spot_ref[0] - spot_ref[1] * (columns // rows)
    for i in range(columns // rows):
        here = jnp.where(part == i, 1.0, 0.0)
        part_ref[i * pieces:(i + 1) * pieces, columns:columns + LANES] = guarded * here
    if part_ref.shape[1] > columns + LANES:
        part_ref[:, columns + LANES:] = jnp.zeros((sectors, LANES), jnp.float32)
        part_ref[:pieces, columns + LANES:] = income


def send_phi(totals_ref, part_ref, send_ref):
    sectors, _, columns = totals_ref.shape
    for j in range(sectors):
        for k in range(columns // LANES):
            lanes = slice(k * LANES, (k + 1) * LANES)
            part_ref[j:j + 1, lanes] = jnp.sum(totals_ref[j, :, lanes], axis=0, keepdims=True)
    part = part_ref[...]
    for copy in range(send_ref.shape[0]):
        send_ref[copy] = part


def first_phi_kernel(spot_ref, slope_ref, productivity_ref, workers_ref, wage_ref, cost_in_ref, send_ref, spread_ref, trade_ref, totals_ref, supply_ref, part_ref, cost_ref, arrived):
    sectors, rows = productivity_ref.shape
    columns = cost_ref.shape[1]
    batch, height = rows // arrived.shape[0], 32
    copies = []
    for i in range(arrived.shape[0]):
        some = pl.ds(i * batch, batch)
        copies.append(pltpu.make_async_copy(cost_in_ref.at[some], cost_ref.at[some], arrived.at[i]))
        copies[-1].start()
    prepare(spot_ref, slope_ref, columns, productivity_ref, workers_ref, wage_ref[...], part_ref, spread_ref, supply_ref)
    slopes = [-slope_ref[j] for j in range(sectors)]
    totals_ref[...] = jnp.zeros_like(totals_ref)

    def step(block, carry):
        at = pl.ds(pl.multiple_of(block * height, height), height)
        for k in range(columns // LANES):
            lanes = slice(k * LANES, (k + 1) * LANES)
            cost = cost_ref[at, lanes].astype(jnp.float32)
            for j in range(sectors):
                trade = jnp.exp(cost * slopes[j])
                trade_ref[j, at, lanes] = trade
                term = trade * spread_ref[at, j * LANES:(j + 1) * LANES]
                totals_ref[j, :, lanes] += tree_sum([term[r:r + 8] for r in range(0, height, 8)])
        return carry

    for i, copy in enumerate(copies):
        copy.wait()
        lax.fori_loop(i * batch // height, (i + 1) * batch // height, step, 0)
    send_phi(totals_ref, part_ref, send_ref)


def phi_kernel(gain, spot_ref, slope_ref, trade_ref, productivity_ref, workers_ref, wage_ref, sales_ref, send_ref, spread_ref, new_wage_ref, totals_ref, supply_ref, part_ref):
    sectors, rows, columns = trade_ref.shape
    blocks = columns // LANES
    wage = next_wage(wage_ref, workers_ref, sales_ref, gain)
    new_wage_ref[...] = wage
    prepare(spot_ref, slope_ref, columns, productivity_ref, workers_ref, wage, part_ref, spread_ref, supply_ref)
    for j in range(sectors):
        def step(block, totals):
            at = pl.ds(pl.multiple_of(block * 8, 8), 8)
            weight = spread_ref[at, j * LANES:(j + 1) * LANES]
            return tuple(totals[k] + trade_ref[j, at, k * LANES:(k + 1) * LANES] * weight for k in range(blocks))

        zero = jnp.zeros((8, LANES), jnp.float32)
        totals = lax.fori_loop(0, rows // 8, step, (zero,) * blocks, unroll=16)
        for k in range(blocks):
            totals_ref[j, :, k * LANES:(k + 1) * LANES] = totals[k]
    send_phi(totals_ref, part_ref, send_ref)


def sum_kernel(got_ref, send_ref):
    total = jnp.sum(got_ref[...], axis=0)
    for copy in range(send_ref.shape[0]):
        send_ref[copy] = total


def sales_kernel(last, cells, slope_ref, trade_ref, spread_ref, preference_ref, got_ref, send_ref, *rest):
    total_ref, ratio_ref, sums_ref = rest[-3:]
    sectors, rows, columns = trade_ref.shape
    blocks = columns // LANES
    sums_ref[...] = jnp.sum(got_ref[...], axis=0)
    preference = preference_ref[...]
    share = preference / jnp.sum(preference, axis=0, keepdims=True)
    for k in range(blocks):
        lanes = slice(k * LANES, (k + 1) * LANES)
        phi = sums_ref[:, lanes]
        ratio = share[:, lanes] * sums_ref[k:k + 1, columns:columns + LANES] / phi
        ratio_ref[:, lanes] = jnp.where(phi < LARGEST, ratio, jnp.nan)
    if sums_ref.shape[1] > columns + LANES:
        centred = CENTRE * cells / total_of(sums_ref[:, columns + LANES:])
        ratio_ref[...] *= centred * centred
    if last:
        slopes = pick(slope_ref, sectors)
        for k in range(blocks):
            lanes = slice(k * LANES, (k + 1) * LANES)
            rest[0][:, lanes] = -jnp.log(sums_ref[:, lanes]) / slopes
    for j in range(sectors):
        ratios = [
            jnp.broadcast_to(ratio_ref[j:j + 1, k * LANES:(k + 1) * LANES], (8, LANES))
            for k in range(blocks)
        ]

        def step(block, carry):
            at = pl.ds(pl.multiple_of(block * 8, 8), 8)
            terms = [trade_ref[j, at, k * LANES:(k + 1) * LANES] * ratios[k] for k in range(blocks)]
            total = tree_sum(terms) * spread_ref[at, j * LANES:(j + 1) * LANES]
            total_ref[at, :] = total if j == 0 else total_ref[at, :] + total
            return carry

        lax.fori_loop(0, rows // 8, step, 0, unroll=8)
    for p in range(rows // LANES):
        piece = jnp.sum(jnp.transpose(total_ref[p * LANES:(p + 1) * LANES, :]), axis=0, keepdims=True)
        send_ref[:, p, :] = jnp.broadcast_to(piece, (send_ref.shape[0], LANES))


def settle_kernel(workers_ref, wage_ref, sales_ref, raw_ref, send_ref):
    raw = next_wage(wage_ref, workers_ref, sales_ref)
    raw_ref[...] = raw
    copies = send_ref.shape[0]
    for row, wage in enumerate((raw, wage_ref[...])):
        world = jnp.sum(wage * workers_ref[...], axis=0, keepdims=True)
        send_ref[:, row, :] = jnp.broadcast_to(world, (copies, LANES))


def finish_kernel(cells, raw_ref, price_ref, got_ref, wage_ref, log_price_ref, world_ref):
    sums = jnp.sum(jnp.sum(got_ref[...], axis=0), axis=1, keepdims=True)
    wage_ref[...] = raw_ref[...] * (cells / sums[0:1])
    log_price_ref[...] = price_ref[...] + jnp.log(cells / sums[1:2])
    world_ref[...] = jnp.broadcast_to(sums[0:1], (1, LANES))


VM = pl.BlockSpec(memory_space=pltpu.VMEM)
SM = pl.BlockSpec(memory_space=pltpu.SMEM)


def call(body, out_shape, scalars, arrays, scratch=(), in_place=()):
    return pl.pallas_call(
        body,
        out_shape=tuple(out_shape),
        in_specs=[SM] * len(scalars) + [VM] * len(arrays) + [pl.BlockSpec(memory_space=pl.ANY)] * len(in_place),
        out_specs=(VM,) * len(out_shape),
        scratch_shapes=[pltpu.VMEM(s, jnp.float32) if isinstance(s, tuple) else s for s in scratch],
        compiler_params=pltpu.CompilerParams(vmem_limit_bytes=16 << 20),
    )(*scalars, *arrays, *in_place)


def exchange(x, axis, groups=None):
    return lax.all_to_all(x, axis, 0, 0, tiled=True, axis_index_groups=groups)


def careful(log_cost, elasticity, productivity, preference, workers, start_wage):
    rows = log_cost.shape[0]
    columns = log_cost.shape[1]
    cells = rows * lax.axis_size("orig")
    spend_share = preference / jnp.sum(preference, axis=0, keepdims=True)

    def settle(raw_wage, wanted):
        local_income = None
        world_income = lax.psum(jnp.sum(raw_wage * workers), "orig")
        factor = cells / world_income
        wage = raw_wage * factor
        if wanted:
            incomes = lax.all_gather(wage * workers, "orig", axis=0, tiled=True)
            local_income = lax.dynamic_slice_in_dim(
                incomes, lax.axis_index("dest") * columns, columns
            )
        return (wage, local_income)

    def kernel_of(slope):
        return jnp.exp(-slope * log_cost.astype(jnp.float32))

    def phi_term(pair):
        return jnp.dot(pair[1], kernel_of(pair[0]), precision=lax.Precision.HIGHEST)

    def sales_term(pair):
        return jnp.dot(kernel_of(pair[0]), pair[1], precision=lax.Precision.HIGHEST)

    wage, dest_income = settle(start_wage, True)
    for step in range(ITERS):
        supply = productivity * jnp.exp(-elasticity[:, None] * jnp.log(wage)[None, :])
        spending = spend_share * dest_income[None, :]
        partial_phi = lax.map(phi_term, (elasticity, supply))
        price_part = lax.psum_scatter(partial_phi, "orig", scatter_dimension=1, tiled=True)
        part_width = price_part.shape[1]
        own_spending = lax.dynamic_slice_in_dim(
            spending, lax.axis_index("orig") * part_width, part_width, 1
        )
        ratio, log_price = (
            lax.all_gather(own_spending / price_part, "orig", axis=1, tiled=True),
            lax.all_gather(-jnp.log(price_part) / elasticity[:, None], "orig", axis=1, tiled=True),
        )
        partial_sales = lax.map(sales_term, (elasticity, ratio))
        sector_sales = lax.psum(partial_sales, "dest")
        revenue = jnp.sum(supply * sector_sales, axis=0)
        raw_wage = wage * jnp.sqrt(revenue / (wage * workers))
        wage, dest_income = settle(raw_wage, step + 1 < ITERS)
    return (wage, log_price)


def fast(log_cost, elasticity, productivity, preference, workers, start_wage):
    sectors, rows = productivity.shape
    columns = log_cost.shape[1]
    across, along = lax.axis_size("orig"), lax.axis_size("dest")
    cells = float(rows * across)
    pieces = rows // LANES
    outer = across // INNER
    by_inner = [[i * INNER + j for j in range(INNER)] for i in range(outer)]
    by_outer = [[i * INNER + j for i in range(outer)] for j in range(INNER)]
    spot = jnp.stack([lax.axis_index("orig"), lax.axis_index("dest")]).astype(jnp.int32)
    workers = workers.reshape(pieces, LANES)
    wage = start_wage.reshape(pieces, LANES)
    sales = trade = None
    for step in range(ITERS):
        last = step + 1 == ITERS
        width = columns + (2 if step == 0 else 1) * LANES
        outs = [f32(outer, sectors, width), f32(rows, sectors * LANES)]
        scratch = [(sectors, 8, columns), (sectors, rows), (sectors, width)]
        if step == 0:
            send, spread, trade = call(
                first_phi_kernel, outs + [f32(sectors, rows, columns)], [spot, elasticity],
                [productivity, workers, wage],
                scratch + [pltpu.VMEM(log_cost.shape, log_cost.dtype), pltpu.SemaphoreType.DMA((2,))],
                [log_cost],
            )
        else:
            send, spread, wage = call(
                functools.partial(phi_kernel, 1.0 if step == 1 else GAIN),
                outs + [f32(pieces, LANES)], [spot, elasticity],
                [trade, productivity, workers, wage, sales], scratch,
            )
        got = exchange(send, "orig", by_outer)
        send, = call(sum_kernel, [f32(INNER, sectors, width)], [], [got])
        got = exchange(send, "orig", by_inner)
        made = call(
            functools.partial(sales_kernel, last, cells),
            [f32(along, pieces, LANES)] + ([f32(sectors, columns)] if last else []),
            [elasticity],
            [trade, spread, preference, got],
            [(rows, LANES), (sectors, columns), (sectors, width)],
        )
        sales = exchange(made[0], "dest")
    raw, send = call(settle_kernel, [f32(pieces, LANES), f32(across, 2, LANES)], [], [workers, wage, sales])
    got = exchange(send, "orig")
    wage, log_price, world = call(
        functools.partial(finish_kernel, cells),
        [f32(pieces, LANES), f32(sectors, columns), f32(1, LANES)], [], [raw, made[1], got],
    )
    return wage.reshape(rows), log_price, world[0, 0]


def on_device(*args):
    wage, log_price, world = fast(*args)
    return lax.cond(jnp.isfinite(world), lambda: (wage, log_price), lambda: careful(*args))


def solution(mesh):
    return jax.shard_map(
        on_device,
        mesh=mesh,
        in_specs=(P("orig", "dest"), P(), P(None, "orig"), P(None, "dest"), P("orig"), P("orig")),
        out_specs=(P("orig"), P(None, "dest")),
        check_vma=False,
    )
```

```python
import functools

import jax
import jax.numpy as jnp
from jax import lax
from jax.experimental import pallas as pl
from jax.experimental.pallas import tpu as pltpu
from jax.sharding import PartitionSpec as P

ITERS = 3
LANES = 128
CENTRE = 1024.0
GAIN = 2.0
INNER = 8
SMALLEST, LARGEST = 1e-32, 1e30


def f32(*shape):
    return jax.ShapeDtypeStruct(shape, jnp.float32)


def tree_sum(terms):
    while len(terms) > 1:
        terms = [a + b for a, b in zip(terms[::2], terms[1::2])]
    return terms[0]


def pick(vector_ref, count):
    row = lax.broadcasted_iota(jnp.int32, (count, LANES), 0)
    out = jnp.zeros((count, LANES), jnp.float32)
    for j in range(count):
        out = jnp.where(row == j, vector_ref[j], out)
    return out


def total_of(x):
    return jnp.sum(jnp.sum(x, axis=0, keepdims=True), axis=1, keepdims=True)


def next_wage(wage_ref, workers_ref, sales_ref, gain=1.0):
    wage, workers = wage_ref[...], workers_ref[...]
    revenue = jnp.sum(sales_ref[...], axis=0)
    return wage * gain * jnp.sqrt(revenue / (wage * workers))


def supply_of(slopes, productivity_ref, wage):
    log_wage = jnp.log(wage)
    pieces = wage.shape[0]
    return [
        productivity_ref[:, p * LANES:(p + 1) * LANES] * jnp.exp(-slopes * log_wage[p:p + 1])
        for p in range(pieces)
    ]


def spread_over_lanes(supply_ref, spread_ref):
    sectors = supply_ref.shape[0]
    row = lax.broadcasted_iota(jnp.int32, (sectors, sectors * LANES), 0)
    lane = lax.broadcasted_iota(jnp.int32, (sectors, sectors * LANES), 1)
    ones = jnp.where((lane >= row * LANES) & (lane < (row + 1) * LANES), 1.0, 0.0).astype(jnp.bfloat16)
    rest, terms = supply_ref[...], []
    for _ in range(3):
        terms.append(rest.astype(jnp.bfloat16))
        rest = rest - terms[-1].astype(jnp.float32)
    spread_ref[...] = lax.dot_general(
        jnp.concatenate(terms, axis=0), jnp.concatenate([ones] * 3, axis=0), (((0,), (0,)), ((), ())),
        preferred_element_type=jnp.float32,
    )


def prepare(slopes, here, columns, productivity_ref, workers_ref, wage, part_ref, spread_ref, supply_ref):
    sectors, rows = productivity_ref.shape
    pieces = rows // LANES
    supply = supply_of(slopes, productivity_ref, wage)
    for p in range(pieces):
        supply_ref[:, p * LANES:(p + 1) * LANES] = supply[p]
    spread_over_lanes(supply_ref, spread_ref)
    least = functools.reduce(jnp.minimum, supply)
    least = jnp.min(jnp.min(least, axis=0, keepdims=True), axis=1, keepdims=True)
    income = wage * workers_ref[...]
    guarded = jnp.where(least > SMALLEST, income, jnp.nan)
    for i in range(columns // rows):
        part_ref[i * pieces:(i + 1) * pieces, columns:columns + LANES] = guarded * here[i:i + 1]
    if part_ref.shape[1] > columns + LANES:
        part_ref[:, columns + LANES:] = jnp.zeros((sectors, LANES), jnp.float32)
        part_ref[:pieces, columns + LANES:] = income


def send_phi(totals_ref, part_ref, send_ref):
    sectors, _, columns = totals_ref.shape
    for j in range(sectors):
        for k in range(columns // LANES):
            lanes = slice(k * LANES, (k + 1) * LANES)
            part_ref[j:j + 1, lanes] = jnp.sum(totals_ref[j, :, lanes], axis=0, keepdims=True)
    part = part_ref[...]
    for copy in range(send_ref.shape[0]):
        send_ref[copy] = part


def first_phi_kernel(
    spot_ref, slope_ref, cost_in_ref, productivity_in_ref, workers_in_ref, wage_in_ref,
    send_ref, spread_ref, trade_ref, facts_ref,
    totals_ref, supply_ref, part_ref, cost_ref, productivity_ref, workers_ref, wage_ref, arrived, brought,
):
    sectors, rows = productivity_ref.shape
    columns = cost_ref.shape[1]
    batch, height = rows // arrived.shape[0], 32
    small = [
        pltpu.make_async_copy(given, held, brought.at[i])
        for i, (given, held) in enumerate(
            ((wage_in_ref, wage_ref), (productivity_in_ref, productivity_ref), (workers_in_ref, workers_ref))
        )
    ]
    copies = []
    for i in range(arrived.shape[0]):
        some = pl.ds(i * batch, batch)
        copies.append(pltpu.make_async_copy(cost_in_ref.at[some], cost_ref.at[some], arrived.at[i]))
    for copy in small + copies:
        copy.start()
    part = spot_ref[0] - spot_ref[1] * (columns // rows)
    facts_ref[:sectors, :] = pick(slope_ref, sectors)
    row = lax.broadcasted_iota(jnp.int32, (sectors, LANES), 0)
    facts_ref[sectors:, :] = jnp.where(row == part, 1.0, 0.0)
    for copy in small:
        copy.wait()
    facts = facts_ref[...]
    prepare(facts[:sectors], facts[sectors:], columns, productivity_ref, workers_ref, wage_ref[...], part_ref, spread_ref, supply_ref)
    slopes = [-slope_ref[j] for j in range(sectors)]
    totals_ref[...] = jnp.zeros_like(totals_ref)

    def step(block, carry):
        at = pl.ds(pl.multiple_of(block * height, height), height)
        for k in range(columns // LANES):
            lanes = slice(k * LANES, (k + 1) * LANES)
            cost = cost_ref[at, lanes].astype(jnp.float32)
            for j in range(sectors):
                trade = jnp.exp(cost * slopes[j])
                trade_ref[j, at, lanes] = trade
                term = trade * spread_ref[at, j * LANES:(j + 1) * LANES]
                totals_ref[j, :, lanes] += tree_sum([term[r:r + 8] for r in range(0, height, 8)])
        return carry

    for i, copy in enumerate(copies):
        copy.wait()
        lax.fori_loop(i * batch // height, (i + 1) * batch // height, step, 0)
    send_phi(totals_ref, part_ref, send_ref)


def phi_kernel(gain, facts_ref, trade_ref, productivity_ref, workers_ref, wage_ref, sales_ref, send_ref, spread_ref, new_wage_ref, totals_ref, supply_ref, part_ref):
    sectors, rows, columns = trade_ref.shape
    blocks = columns // LANES
    wage = next_wage(wage_ref, workers_ref, sales_ref, gain)
    new_wage_ref[...] = wage
    prepare(facts_ref[:sectors], facts_ref[sectors:], columns, productivity_ref, workers_ref, wage, part_ref, spread_ref, supply_ref)
    for j in range(sectors):
        def step(block, totals):
            at = pl.ds(pl.multiple_of(block * 8, 8), 8)
            weight = spread_ref[at, j * LANES:(j + 1) * LANES]
            return tuple(totals[k] + trade_ref[j, at, k * LANES:(k + 1) * LANES] * weight for k in range(blocks))

        zero = jnp.zeros((8, LANES), jnp.float32)
        totals = lax.fori_loop(0, rows // 8, step, (zero,) * blocks, unroll=16)
        for k in range(blocks):
            totals_ref[j, :, k * LANES:(k + 1) * LANES] = totals[k]
    send_phi(totals_ref, part_ref, send_ref)


def sum_kernel(got_ref, send_ref):
    total = jnp.sum(got_ref[...], axis=0)
    for copy in range(send_ref.shape[0]):
        send_ref[copy] = total


def sales_kernel(last, cells, facts_ref, trade_ref, spread_ref, preference_ref, got_ref, send_ref, *rest):
    total_ref, ratio_ref, sums_ref = rest[-3:]
    sectors, rows, columns = trade_ref.shape
    blocks = columns // LANES
    sums_ref[...] = jnp.sum(got_ref[...], axis=0)
    preference = preference_ref[...]
    share = preference / jnp.sum(preference, axis=0, keepdims=True)
    for k in range(blocks):
        lanes = slice(k * LANES, (k + 1) * LANES)
        phi = sums_ref[:, lanes]
        ratio = share[:, lanes] * sums_ref[k:k + 1, columns:columns + LANES] / phi
        ratio_ref[:, lanes] = jnp.where(phi < LARGEST, ratio, jnp.nan)
    if sums_ref.shape[1] > columns + LANES:
        centred = CENTRE * cells / total_of(sums_ref[:, columns + LANES:])
        ratio_ref[...] *= centred * centred
    if last:
        slopes = facts_ref[:sectors]
        for k in range(blocks):
            lanes = slice(k * LANES, (k + 1) * LANES)
            rest[0][:, lanes] = -jnp.log(sums_ref[:, lanes]) / slopes
    for j in range(sectors):
        ratios = [
            jnp.broadcast_to(ratio_ref[j:j + 1, k * LANES:(k + 1) * LANES], (8, LANES))
            for k in range(blocks)
        ]

        def step(block, carry):
            at = pl.ds(pl.multiple_of(block * 8, 8), 8)
            terms = [trade_ref[j, at, k * LANES:(k + 1) * LANES] * ratios[k] for k in range(blocks)]
            total = tree_sum(terms) * spread_ref[at, j * LANES:(j + 1) * LANES]
            total_ref[at, :] = total if j == 0 else total_ref[at, :] + total
            return carry

        lax.fori_loop(0, rows // 8, step, 0, unroll=8)
    for p in range(rows // LANES):
        piece = jnp.sum(jnp.transpose(total_ref[p * LANES:(p + 1) * LANES, :]), axis=0, keepdims=True)
        send_ref[:, p, :] = jnp.broadcast_to(piece, (send_ref.shape[0], LANES))


def settle_kernel(workers_ref, wage_ref, sales_ref, raw_ref, send_ref):
    raw = next_wage(wage_ref, workers_ref, sales_ref)
    raw_ref[...] = raw
    copies = send_ref.shape[0]
    for row, wage in enumerate((raw, wage_ref[...])):
        world = jnp.sum(wage * workers_ref[...], axis=0, keepdims=True)
        send_ref[:, row, :] = jnp.broadcast_to(world, (copies, LANES))


def finish_kernel(cells, raw_ref, price_ref, got_ref, wage_ref, log_price_ref, world_ref):
    sums = jnp.sum(jnp.sum(got_ref[...], axis=0), axis=1, keepdims=True)
    wage_ref[...] = raw_ref[...] * (cells / sums[0:1])
    log_price_ref[...] = price_ref[...] + jnp.log(cells / sums[1:2])
    world_ref[...] = jnp.broadcast_to(sums[0:1], (1, LANES))


VM = pl.BlockSpec(memory_space=pltpu.VMEM)
SM = pl.BlockSpec(memory_space=pltpu.SMEM)


def call(body, out_shape, scalars, arrays, scratch=(), in_place=()):
    return pl.pallas_call(
        body,
        out_shape=tuple(out_shape),
        in_specs=[SM] * len(scalars) + [VM] * len(arrays) + [pl.BlockSpec(memory_space=pl.ANY)] * len(in_place),
        out_specs=(VM,) * len(out_shape),
        scratch_shapes=[pltpu.VMEM(s, jnp.float32) if isinstance(s, tuple) else s for s in scratch],
        compiler_params=pltpu.CompilerParams(vmem_limit_bytes=16 << 20),
    )(*scalars, *arrays, *in_place)


def exchange(x, axis, groups=None):
    return lax.all_to_all(x, axis, 0, 0, tiled=True, axis_index_groups=groups)


def careful(log_cost, elasticity, productivity, preference, workers, start_wage):
    rows = log_cost.shape[0]
    columns = log_cost.shape[1]
    cells = rows * lax.axis_size("orig")
    spend_share = preference / jnp.sum(preference, axis=0, keepdims=True)

    def settle(raw_wage, wanted):
        local_income = None
        world_income = lax.psum(jnp.sum(raw_wage * workers), "orig")
        factor = cells / world_income
        wage = raw_wage * factor
        if wanted:
            incomes = lax.all_gather(wage * workers, "orig", axis=0, tiled=True)
            local_income = lax.dynamic_slice_in_dim(
                incomes, lax.axis_index("dest") * columns, columns
            )
        return (wage, local_income)

    def kernel_of(slope):
        return jnp.exp(-slope * log_cost.astype(jnp.float32))

    def phi_term(pair):
        return jnp.dot(pair[1], kernel_of(pair[0]), precision=lax.Precision.HIGHEST)

    def sales_term(pair):
        return jnp.dot(kernel_of(pair[0]), pair[1], precision=lax.Precision.HIGHEST)

    wage, dest_income = settle(start_wage, True)
    for step in range(ITERS):
        supply = productivity * jnp.exp(-elasticity[:, None] * jnp.log(wage)[None, :])
        spending = spend_share * dest_income[None, :]
        partial_phi = lax.map(phi_term, (elasticity, supply))
        price_part = lax.psum_scatter(partial_phi, "orig", scatter_dimension=1, tiled=True)
        part_width = price_part.shape[1]
        own_spending = lax.dynamic_slice_in_dim(
            spending, lax.axis_index("orig") * part_width, part_width, 1
        )
        ratio, log_price = (
            lax.all_gather(own_spending / price_part, "orig", axis=1, tiled=True),
            lax.all_gather(-jnp.log(price_part) / elasticity[:, None], "orig", axis=1, tiled=True),
        )
        partial_sales = lax.map(sales_term, (elasticity, ratio))
        sector_sales = lax.psum(partial_sales, "dest")
        revenue = jnp.sum(supply * sector_sales, axis=0)
        raw_wage = wage * jnp.sqrt(revenue / (wage * workers))
        wage, dest_income = settle(raw_wage, step + 1 < ITERS)
    return (wage, log_price)


def fast(log_cost, elasticity, productivity, preference, workers, start_wage):
    sectors, rows = productivity.shape
    columns = log_cost.shape[1]
    across, along = lax.axis_size("orig"), lax.axis_size("dest")
    cells = float(rows * across)
    pieces = rows // LANES
    outer = across // INNER
    by_inner = [[i * INNER + j for j in range(INNER)] for i in range(outer)]
    by_outer = [[i * INNER + j for i in range(outer)] for j in range(INNER)]
    spot = jnp.stack([lax.axis_index("orig"), lax.axis_index("dest")]).astype(jnp.int32)
    workers = workers.reshape(pieces, LANES)
    wage = start_wage.reshape(pieces, LANES)
    sales = trade = None
    for step in range(ITERS):
        last = step + 1 == ITERS
        width = columns + (2 if step == 0 else 1) * LANES
        outs = [f32(outer, sectors, width), f32(rows, sectors * LANES)]
        scratch = [(sectors, 8, columns), (sectors, rows), (sectors, width)]
        if step == 0:
            send, spread, trade, facts = call(
                first_phi_kernel, outs + [f32(sectors, rows, columns), f32(2 * sectors, LANES)], [spot, elasticity], [],
                scratch + [pltpu.VMEM(log_cost.shape, log_cost.dtype), (sectors, rows), (pieces, LANES), (pieces, LANES)]
                + [pltpu.SemaphoreType.DMA((2,)), pltpu.SemaphoreType.DMA((3,))],
                [log_cost, productivity, workers, wage],
            )
        else:
            send, spread, wage = call(
                functools.partial(phi_kernel, 1.0 if step == 1 else GAIN),
                outs + [f32(pieces, LANES)], [],
                [facts, trade, productivity, workers, wage, sales], scratch,
            )
        got = exchange(send, "orig", by_outer)
        send, = call(sum_kernel, [f32(INNER, sectors, width)], [], [got])
        got = exchange(send, "orig", by_inner)
        made = call(
            functools.partial(sales_kernel, last, cells),
            [f32(along, pieces, LANES)] + ([f32(sectors, columns)] if last else []),
            [],
            [facts, trade, spread, preference, got],
            [(rows, LANES), (sectors, columns), (sectors, width)],
        )
        sales = exchange(made[0], "dest")
    raw, send = call(settle_kernel, [f32(pieces, LANES), f32(across, 2, LANES)], [], [workers, wage, sales])
    got = exchange(send, "orig")
    wage, log_price, world = call(
        functools.partial(finish_kernel, cells),
        [f32(pieces, LANES), f32(sectors, columns), f32(1, LANES)], [], [raw, made[1], got],
    )
    return wage.reshape(rows), log_price, world[0, 0]


def on_device(*args):
    wage, log_price, world = fast(*args)
    return lax.cond(jnp.isfinite(world), lambda: (wage, log_price), lambda: careful(*args))


def solution(mesh):
    return jax.shard_map(
        on_device,
        mesh=mesh,
        in_specs=(P("orig", "dest"), P(), P(None, "orig"), P(None, "dest"), P("orig"), P("orig")),
        out_specs=(P("orig"), P(None, "dest")),
        check_vma=False,
    )
```

```python
import functools

import jax
import jax.numpy as jnp
from jax import lax
from jax.experimental import pallas as pl
from jax.experimental.pallas import tpu as pltpu
from jax.sharding import PartitionSpec as P

ITERS = 3
LANES = 128
CENTRE = 1024.0
GAIN = 2.0
INNER = 8
SMALLEST, LARGEST = 1e-32, 1e30


def f32(*shape):
    return jax.ShapeDtypeStruct(shape, jnp.float32)


def tree_sum(terms):
    while len(terms) > 1:
        terms = [a + b for a, b in zip(terms[::2], terms[1::2])]
    return terms[0]


def pick(vector_ref, count):
    row = lax.broadcasted_iota(jnp.int32, (count, LANES), 0)
    out = jnp.zeros((count, LANES), jnp.float32)
    for j in range(count):
        out = jnp.where(row == j, vector_ref[j], out)
    return out


def total_of(x):
    return jnp.sum(jnp.sum(x, axis=0, keepdims=True), axis=1, keepdims=True)


def next_wage(wage_ref, workers_ref, sales_ref, gain=1.0):
    wage, workers = wage_ref[...], workers_ref[...]
    revenue = jnp.sum(sales_ref[...], axis=0)
    return wage * gain * jnp.sqrt(revenue / (wage * workers))


def supply_of(slopes, productivity_ref, wage):
    log_wage = jnp.log(wage)
    pieces = wage.shape[0]
    return [
        productivity_ref[:, p * LANES:(p + 1) * LANES] * jnp.exp(-slopes * log_wage[p:p + 1])
        for p in range(pieces)
    ]


def spread_over_lanes(supply_ref, spread_ref):
    sectors = supply_ref.shape[0]
    row = lax.broadcasted_iota(jnp.int32, (sectors, sectors * LANES), 0)
    lane = lax.broadcasted_iota(jnp.int32, (sectors, sectors * LANES), 1)
    ones = jnp.where((lane >= row * LANES) & (lane < (row + 1) * LANES), 1.0, 0.0).astype(jnp.bfloat16)
    rest, terms = supply_ref[...], []
    for _ in range(3):
        terms.append(rest.astype(jnp.bfloat16))
        rest = rest - terms[-1].astype(jnp.float32)
    spread_ref[...] = lax.dot_general(
        jnp.concatenate(terms, axis=0), jnp.concatenate([ones] * 3, axis=0), (((0,), (0,)), ((), ())),
        preferred_element_type=jnp.float32,
    )


def prepare(slopes, here, columns, productivity_ref, workers_ref, wage, part_ref, spread_ref, supply_ref):
    sectors, rows = productivity_ref.shape
    pieces = rows // LANES
    supply = supply_of(slopes, productivity_ref, wage)
    for p in range(pieces):
        supply_ref[:, p * LANES:(p + 1) * LANES] = supply[p]
    spread_over_lanes(supply_ref, spread_ref)
    least = functools.reduce(jnp.minimum, supply)
    least = jnp.min(jnp.min(least, axis=0, keepdims=True), axis=1, keepdims=True)
    income = wage * workers_ref[...]
    guarded = jnp.where(least > SMALLEST, income, jnp.nan)
    for i in range(columns // rows):
        part_ref[i * pieces:(i + 1) * pieces, columns:columns + LANES] = guarded * here[i:i + 1]
    if part_ref.shape[1] > columns + LANES:
        part_ref[:, columns + LANES:] = jnp.zeros((sectors, LANES), jnp.float32)
        part_ref[:pieces, columns + LANES:] = income


def send_phi(totals_ref, part_ref, send_ref):
    sectors, _, columns = totals_ref.shape
    for j in range(sectors):
        for k in range(columns // LANES):
            lanes = slice(k * LANES, (k + 1) * LANES)
            part_ref[j:j + 1, lanes] = jnp.sum(totals_ref[j, :, lanes], axis=0, keepdims=True)
    part = part_ref[...]
    for copy in range(send_ref.shape[0]):
        send_ref[copy] = part


def first_phi_kernel(
    spot_ref, slope_ref, cost_in_ref, productivity_in_ref, workers_in_ref, wage_in_ref,
    send_ref, spread_ref, trade_ref, facts_ref,
    totals_ref, supply_ref, part_ref, cost_ref, productivity_ref, workers_ref, wage_ref, arrived, brought,
):
    sectors, rows = productivity_ref.shape
    columns = cost_ref.shape[1]
    batch, height = rows // arrived.shape[0], 32
    small = [
        pltpu.make_async_copy(given, held, brought.at[i])
        for i, (given, held) in enumerate(
            ((wage_in_ref, wage_ref), (productivity_in_ref, productivity_ref), (workers_in_ref, workers_ref))
        )
    ]
    copies = []
    for i in range(arrived.shape[0]):
        some = pl.ds(i * batch, batch)
        copies.append(pltpu.make_async_copy(cost_in_ref.at[some], cost_ref.at[some], arrived.at[i]))
    for copy in small + copies:
        copy.start()
    part = spot_ref[0] - spot_ref[1] * (columns // rows)
    facts_ref[:sectors, :] = pick(slope_ref, sectors)
    row = lax.broadcasted_iota(jnp.int32, (sectors, LANES), 0)
    facts_ref[sectors:, :] = jnp.where(row == part, 1.0, 0.0)
    for copy in small:
        copy.wait()
    facts = facts_ref[...]
    prepare(facts[:sectors], facts[sectors:], columns, productivity_ref, workers_ref, wage_ref[...], part_ref, spread_ref, supply_ref)
    slopes = [-slope_ref[j] for j in range(sectors)]
    totals_ref[...] = jnp.zeros_like(totals_ref)

    def step(block, carry):
        at = pl.ds(pl.multiple_of(block * height, height), height)
        for k in range(columns // LANES):
            lanes = slice(k * LANES, (k + 1) * LANES)
            cost = cost_ref[at, lanes].astype(jnp.float32)
            for j in range(sectors):
                trade = jnp.exp(cost * slopes[j])
                trade_ref[j, at, lanes] = trade
                term = trade * spread_ref[at, j * LANES:(j + 1) * LANES]
                totals_ref[j, :, lanes] += tree_sum([term[r:r + 8] for r in range(0, height, 8)])
        return carry

    for i, copy in enumerate(copies):
        copy.wait()
        lax.fori_loop(i * batch // height, (i + 1) * batch // height, step, 0)
    send_phi(totals_ref, part_ref, send_ref)


def phi_kernel(gain, facts_ref, trade_ref, productivity_ref, workers_ref, wage_ref, sales_ref, send_ref, spread_ref, new_wage_ref, totals_ref, supply_ref, part_ref):
    sectors, rows, columns = trade_ref.shape
    blocks = columns // LANES
    wage = next_wage(wage_ref, workers_ref, sales_ref, gain)
    new_wage_ref[...] = wage
    prepare(facts_ref[:sectors], facts_ref[sectors:], columns, productivity_ref, workers_ref, wage, part_ref, spread_ref, supply_ref)
    for j in range(sectors):
        def step(block, totals):
            at = pl.ds(pl.multiple_of(block * 8, 8), 8)
            weight = spread_ref[at, j * LANES:(j + 1) * LANES]
            return tuple(totals[k] + trade_ref[j, at, k * LANES:(k + 1) * LANES] * weight for k in range(blocks))

        zero = jnp.zeros((8, LANES), jnp.float32)
        totals = lax.fori_loop(0, rows // 8, step, (zero,) * blocks, unroll=16)
        for k in range(blocks):
            totals_ref[j, :, k * LANES:(k + 1) * LANES] = totals[k]
    send_phi(totals_ref, part_ref, send_ref)


def sum_kernel(got_ref, send_ref):
    total = jnp.sum(got_ref[...], axis=0)
    for copy in range(send_ref.shape[0]):
        send_ref[copy] = total


def sales_kernel(last, cells, facts_ref, trade_ref, spread_ref, preference_ref, got_ref, send_ref, *rest):
    total_ref, ratio_ref, sums_ref = rest[-3:]
    sectors, rows, columns = trade_ref.shape
    blocks = columns // LANES
    sums_ref[...] = jnp.sum(got_ref[...], axis=0)
    preference = preference_ref[...]
    share = preference / jnp.sum(preference, axis=0, keepdims=True)
    for k in range(blocks):
        lanes = slice(k * LANES, (k + 1) * LANES)
        phi = sums_ref[:, lanes]
        ratio = share[:, lanes] * sums_ref[k:k + 1, columns:columns + LANES] / phi
        ratio_ref[:, lanes] = jnp.where(phi < LARGEST, ratio, jnp.nan)
    if sums_ref.shape[1] > columns + LANES:
        centred = CENTRE * cells / total_of(sums_ref[:, columns + LANES:])
        ratio_ref[...] *= centred * centred
    if last:
        slopes = facts_ref[:sectors]
        for k in range(blocks):
            lanes = slice(k * LANES, (k + 1) * LANES)
            rest[0][:, lanes] = -jnp.log(sums_ref[:, lanes]) / slopes
    for j in range(sectors):
        ratios = [
            jnp.broadcast_to(ratio_ref[j:j + 1, k * LANES:(k + 1) * LANES], (8, LANES))
            for k in range(blocks)
        ]

        def step(block, carry):
            at = pl.ds(pl.multiple_of(block * 8, 8), 8)
            terms = [trade_ref[j, at, k * LANES:(k + 1) * LANES] * ratios[k] for k in range(blocks)]
            total = tree_sum(terms) * spread_ref[at, j * LANES:(j + 1) * LANES]
            total_ref[at, :] = total if j == 0 else total_ref[at, :] + total
            return carry

        lax.fori_loop(0, rows // 8, step, 0, unroll=8)
    for p in range(rows // LANES):
        piece = jnp.sum(jnp.transpose(total_ref[p * LANES:(p + 1) * LANES, :]), axis=0, keepdims=True)
        send_ref[:, p, :] = jnp.broadcast_to(piece, (send_ref.shape[0], LANES))


def settle_kernel(workers_ref, wage_ref, sales_ref, raw_ref, send_ref):
    raw = next_wage(wage_ref, workers_ref, sales_ref)
    raw_ref[...] = raw
    copies = send_ref.shape[0]
    for row, wage in enumerate((raw, wage_ref[...])):
        world = jnp.sum(wage * workers_ref[...], axis=0, keepdims=True)
        send_ref[:, row, :] = jnp.broadcast_to(world, (copies, LANES))


def finish_kernel(cells, raw_ref, price_ref, got_ref, wage_ref, log_price_ref, world_ref):
    sums = jnp.sum(jnp.sum(got_ref[...], axis=0), axis=1, keepdims=True)
    wage_ref[...] = raw_ref[...] * (cells / sums[0:1])
    log_price_ref[...] = price_ref[...] + jnp.log(cells / sums[1:2])
    world_ref[...] = jnp.broadcast_to(sums[0:1], (1, LANES))


VM = pl.BlockSpec(memory_space=pltpu.VMEM)
SM = pl.BlockSpec(memory_space=pltpu.SMEM)


def call(body, out_shape, scalars, arrays, scratch=(), in_place=()):
    return pl.pallas_call(
        body,
        out_shape=tuple(out_shape),
        in_specs=[SM] * len(scalars) + [VM] * len(arrays) + [pl.BlockSpec(memory_space=pl.ANY)] * len(in_place),
        out_specs=(VM,) * len(out_shape),
        scratch_shapes=[pltpu.VMEM(s, jnp.float32) if isinstance(s, tuple) else s for s in scratch],
        compiler_params=pltpu.CompilerParams(vmem_limit_bytes=16 << 20),
    )(*scalars, *arrays, *in_place)


def exchange(x, axis, groups=None):
    return lax.all_to_all(x, axis, 0, 0, tiled=True, axis_index_groups=groups)


def gather(x, axis):
    return exchange(jnp.broadcast_to(x, (lax.axis_size(axis), *x.shape)), axis)


def careful(log_cost, elasticity, productivity, preference, workers, start_wage):
    rows, columns = log_cost.shape
    sectors = elasticity.shape[0]
    across = lax.axis_size("orig")
    cells, width = rows * across, columns // across
    spend_share = preference / jnp.sum(preference, axis=0, keepdims=True)

    def settle(raw_wage, wanted):
        world_income = jnp.sum(gather(jnp.sum(raw_wage * workers, keepdims=True), "orig"))
        wage = raw_wage * (cells / world_income)
        if not wanted:
            return wage, None
        incomes = gather(wage * workers, "orig").reshape(cells)
        return wage, lax.dynamic_slice_in_dim(incomes, lax.axis_index("dest") * columns, columns)

    def kernel_of(slope):
        return jnp.exp(-slope * log_cost.astype(jnp.float32))

    def phi_term(pair):
        return jnp.dot(pair[1], kernel_of(pair[0]), precision=lax.Precision.HIGHEST)

    def sales_term(pair):
        return jnp.dot(kernel_of(pair[0]), pair[1], precision=lax.Precision.HIGHEST)

    def whole(x):
        return jnp.moveaxis(gather(x, "orig"), 0, 1).reshape(sectors, columns)

    wage, dest_income = settle(start_wage, True)
    for step in range(ITERS):
        supply = productivity * jnp.exp(-elasticity[:, None] * jnp.log(wage)[None, :])
        spending = spend_share * dest_income[None, :]
        partial_phi = lax.map(phi_term, (elasticity, supply)).reshape(sectors, across, width)
        phi = whole(jnp.sum(exchange(jnp.moveaxis(partial_phi, 1, 0), "orig"), axis=0))
        log_price = -jnp.log(phi) / elasticity[:, None]
        partial_sales = lax.map(sales_term, (elasticity, spending / phi))
        revenue = jnp.sum(gather(jnp.sum(supply * partial_sales, axis=0), "dest"), axis=0)
        raw_wage = wage * jnp.sqrt(revenue / (wage * workers))
        wage, dest_income = settle(raw_wage, step + 1 < ITERS)
    return wage, log_price


def fast(log_cost, elasticity, productivity, preference, workers, start_wage):
    sectors, rows = productivity.shape
    columns = log_cost.shape[1]
    across, along = lax.axis_size("orig"), lax.axis_size("dest")
    cells = float(rows * across)
    pieces = rows // LANES
    outer = across // INNER
    by_inner = [[i * INNER + j for j in range(INNER)] for i in range(outer)]
    by_outer = [[i * INNER + j for i in range(outer)] for j in range(INNER)]
    spot = jnp.stack([lax.axis_index("orig"), lax.axis_index("dest")]).astype(jnp.int32)
    workers = workers.reshape(pieces, LANES)
    wage = start_wage.reshape(pieces, LANES)
    sales = trade = None
    for step in range(ITERS):
        last = step + 1 == ITERS
        width = columns + (2 if step == 0 else 1) * LANES
        outs = [f32(outer, sectors, width), f32(rows, sectors * LANES)]
        scratch = [(sectors, 8, columns), (sectors, rows), (sectors, width)]
        if step == 0:
            send, spread, trade, facts = call(
                first_phi_kernel, outs + [f32(sectors, rows, columns), f32(2 * sectors, LANES)], [spot, elasticity], [],
                scratch + [pltpu.VMEM(log_cost.shape, log_cost.dtype), (sectors, rows), (pieces, LANES), (pieces, LANES)]
                + [pltpu.SemaphoreType.DMA((2,)), pltpu.SemaphoreType.DMA((3,))],
                [log_cost, productivity, workers, wage],
            )
        else:
            send, spread, wage = call(
                functools.partial(phi_kernel, 1.0 if step == 1 else GAIN),
                outs + [f32(pieces, LANES)], [],
                [facts, trade, productivity, workers, wage, sales], scratch,
            )
        got = exchange(send, "orig", by_outer)
        send, = call(sum_kernel, [f32(INNER, sectors, width)], [], [got])
        got = exchange(send, "orig", by_inner)
        made = call(
            functools.partial(sales_kernel, last, cells),
            [f32(along, pieces, LANES)] + ([f32(sectors, columns)] if last else []),
            [],
            [facts, trade, spread, preference, got],
            [(rows, LANES), (sectors, columns), (sectors, width)],
        )
        sales = exchange(made[0], "dest")
    raw, send = call(settle_kernel, [f32(pieces, LANES), f32(across, 2, LANES)], [], [workers, wage, sales])
    got = exchange(send, "orig")
    wage, log_price, world = call(
        functools.partial(finish_kernel, cells),
        [f32(pieces, LANES), f32(sectors, columns), f32(1, LANES)], [], [raw, made[1], got],
    )
    return wage.reshape(rows), log_price, world[0, 0]


def on_device(*args):
    wage, log_price, world = fast(*args)
    return lax.cond(jnp.isfinite(world), lambda: (wage, log_price), lambda: careful(*args))


def solution(mesh):
    return jax.shard_map(
        on_device,
        mesh=mesh,
        in_specs=(P("orig", "dest"), P(), P(None, "orig"), P(None, "dest"), P("orig"), P("orig")),
        out_specs=(P("orig"), P(None, "dest")),
        check_vma=False,
    )
```

```python
import functools

import jax
import jax.numpy as jnp
from jax import lax
from jax.experimental import pallas as pl
from jax.experimental.pallas import tpu as pltpu
from jax.sharding import PartitionSpec as P

ITERS = 3
LANES = 128
CENTRE = 1024.0
GAIN = 2.0
INNER = 8
SMALLEST, LARGEST = 1e-32, 1e30


def f32(*shape):
    return jax.ShapeDtypeStruct(shape, jnp.float32)


def tree_sum(terms):
    while len(terms) > 1:
        terms = [a + b for a, b in zip(terms[::2], terms[1::2])]
    return terms[0]


def pick(vector_ref, count):
    row = lax.broadcasted_iota(jnp.int32, (count, LANES), 0)
    out = jnp.zeros((count, LANES), jnp.float32)
    for j in range(count):
        out = jnp.where(row == j, vector_ref[j], out)
    return out


def total_of(x):
    return jnp.sum(jnp.sum(x, axis=0, keepdims=True), axis=1, keepdims=True)


def next_wage(wage_ref, workers_ref, sales_ref, gain=1.0):
    wage, workers = wage_ref[...], workers_ref[...]
    revenue = jnp.sum(sales_ref[...], axis=0)
    return wage * gain * jnp.sqrt(revenue / (wage * workers))


def supply_of(slopes, productivity_ref, wage):
    log_wage = jnp.log(wage)
    pieces = wage.shape[0]
    return [
        productivity_ref[:, p * LANES:(p + 1) * LANES] * jnp.exp(-slopes * log_wage[p:p + 1])
        for p in range(pieces)
    ]


def spread_over_lanes(supply_ref, spread_ref):
    sectors = supply_ref.shape[0]
    row = lax.broadcasted_iota(jnp.int32, (sectors, sectors * LANES), 0)
    lane = lax.broadcasted_iota(jnp.int32, (sectors, sectors * LANES), 1)
    ones = jnp.where((lane >= row * LANES) & (lane < (row + 1) * LANES), 1.0, 0.0).astype(jnp.bfloat16)
    rest, terms = supply_ref[...], []
    for _ in range(3):
        terms.append(rest.astype(jnp.bfloat16))
        rest = rest - terms[-1].astype(jnp.float32)
    spread_ref[...] = lax.dot_general(
        jnp.concatenate(terms, axis=0), jnp.concatenate([ones] * 3, axis=0), (((0,), (0,)), ((), ())),
        preferred_element_type=jnp.float32,
    )


def prepare(slopes, here, columns, productivity_ref, workers_ref, wage, part_ref, spread_ref, supply_ref):
    sectors, rows = productivity_ref.shape
    pieces = rows // LANES
    supply = supply_of(slopes, productivity_ref, wage)
    for p in range(pieces):
        supply_ref[:, p * LANES:(p + 1) * LANES] = supply[p]
    spread_over_lanes(supply_ref, spread_ref)
    least = functools.reduce(jnp.minimum, supply)
    least = jnp.min(jnp.min(least, axis=0, keepdims=True), axis=1, keepdims=True)
    income = wage * workers_ref[...]
    guarded = jnp.where(least > SMALLEST, income, jnp.nan)
    for i in range(columns // rows):
        part_ref[i * pieces:(i + 1) * pieces, columns:columns + LANES] = guarded * here[i:i + 1]
    if part_ref.shape[1] > columns + LANES:
        part_ref[:, columns + LANES:] = jnp.zeros((sectors, LANES), jnp.float32)
        part_ref[:pieces, columns + LANES:] = income


def send_phi(totals_ref, part_ref, send_ref):
    sectors, _, columns = totals_ref.shape
    for j in range(sectors):
        for k in range(columns // LANES):
            lanes = slice(k * LANES, (k + 1) * LANES)
            part_ref[j:j + 1, lanes] = jnp.sum(totals_ref[j, :, lanes], axis=0, keepdims=True)
    part = part_ref[...]
    for copy in range(send_ref.shape[0]):
        send_ref[copy] = part


def first_phi_kernel(
    cost_in_ref, slope_in_ref, productivity_in_ref, workers_in_ref, wage_in_ref,
    send_ref, spread_ref, trade_ref, facts_ref,
    totals_ref, supply_ref, part_ref, cost_ref, slope_ref, productivity_ref, workers_ref, wage_ref, arrived, brought,
):
    sectors, rows = productivity_ref.shape
    columns = cost_ref.shape[1]
    batch, height = rows // arrived.shape[0], 32
    small = [
        pltpu.make_async_copy(given, held, brought.at[i])
        for i, (given, held) in enumerate(
            ((slope_in_ref, slope_ref), (wage_in_ref, wage_ref), (productivity_in_ref, productivity_ref), (workers_in_ref, workers_ref))
        )
    ]
    copies = []
    for i in range(arrived.shape[0]):
        some = pl.ds(i * batch, batch)
        copies.append(pltpu.make_async_copy(cost_in_ref.at[some], cost_ref.at[some], arrived.at[i]))
    for copy in small + copies:
        copy.start()
    part = lax.axis_index("orig") - lax.axis_index("dest") * (columns // rows)
    row = lax.broadcasted_iota(jnp.int32, (sectors, LANES), 0)
    facts_ref[sectors:, :] = jnp.where(row == part, 1.0, 0.0)
    for copy in small:
        copy.wait()
    facts_ref[:sectors, :] = pick(slope_ref, sectors)
    facts = facts_ref[...]
    prepare(facts[:sectors], facts[sectors:], columns, productivity_ref, workers_ref, wage_ref[...], part_ref, spread_ref, supply_ref)
    slopes = [-slope_ref[j] for j in range(sectors)]
    totals_ref[...] = jnp.zeros_like(totals_ref)

    def step(block, carry):
        at = pl.ds(pl.multiple_of(block * height, height), height)
        for k in range(columns // LANES):
            lanes = slice(k * LANES, (k + 1) * LANES)
            cost = cost_ref[at, lanes].astype(jnp.float32)
            for j in range(sectors):
                trade = jnp.exp(cost * slopes[j])
                trade_ref[j, at, lanes] = trade
                term = trade * spread_ref[at, j * LANES:(j + 1) * LANES]
                totals_ref[j, :, lanes] += tree_sum([term[r:r + 8] for r in range(0, height, 8)])
        return carry

    for i, copy in enumerate(copies):
        copy.wait()
        lax.fori_loop(i * batch // height, (i + 1) * batch // height, step, 0)
    send_phi(totals_ref, part_ref, send_ref)


def phi_kernel(gain, facts_ref, trade_ref, productivity_ref, workers_ref, wage_ref, sales_ref, send_ref, spread_ref, new_wage_ref, totals_ref, supply_ref, part_ref):
    sectors, rows, columns = trade_ref.shape
    blocks = columns // LANES
    wage = next_wage(wage_ref, workers_ref, sales_ref, gain)
    new_wage_ref[...] = wage
    prepare(facts_ref[:sectors], facts_ref[sectors:], columns, productivity_ref, workers_ref, wage, part_ref, spread_ref, supply_ref)
    for j in range(sectors):
        def step(block, totals):
            at = pl.ds(pl.multiple_of(block * 8, 8), 8)
            weight = spread_ref[at, j * LANES:(j + 1) * LANES]
            return tuple(totals[k] + trade_ref[j, at, k * LANES:(k + 1) * LANES] * weight for k in range(blocks))

        zero = jnp.zeros((8, LANES), jnp.float32)
        totals = lax.fori_loop(0, rows // 8, step, (zero,) * blocks, unroll=16)
        for k in range(blocks):
            totals_ref[j, :, k * LANES:(k + 1) * LANES] = totals[k]
    send_phi(totals_ref, part_ref, send_ref)


def sum_kernel(got_ref, send_ref):
    total = jnp.sum(got_ref[...], axis=0)
    for copy in range(send_ref.shape[0]):
        send_ref[copy] = total


def sales_kernel(last, cells, facts_ref, trade_ref, spread_ref, preference_ref, got_ref, send_ref, *rest):
    total_ref, ratio_ref, sums_ref = rest[-3:]
    sectors, rows, columns = trade_ref.shape
    blocks = columns // LANES
    sums_ref[...] = jnp.sum(got_ref[...], axis=0)
    preference = preference_ref[...]
    share = preference / jnp.sum(preference, axis=0, keepdims=True)
    for k in range(blocks):
        lanes = slice(k * LANES, (k + 1) * LANES)
        phi = sums_ref[:, lanes]
        ratio = share[:, lanes] * sums_ref[k:k + 1, columns:columns + LANES] / phi
        ratio_ref[:, lanes] = jnp.where(phi < LARGEST, ratio, jnp.nan)
    if sums_ref.shape[1] > columns + LANES:
        centred = CENTRE * cells / total_of(sums_ref[:, columns + LANES:])
        ratio_ref[...] *= centred * centred
    if last:
        slopes = facts_ref[:sectors]
        for k in range(blocks):
            lanes = slice(k * LANES, (k + 1) * LANES)
            rest[0][:, lanes] = -jnp.log(sums_ref[:, lanes]) / slopes
    for j in range(sectors):
        ratios = [
            jnp.broadcast_to(ratio_ref[j:j + 1, k * LANES:(k + 1) * LANES], (8, LANES))
            for k in range(blocks)
        ]

        def step(block, carry):
            at = pl.ds(pl.multiple_of(block * 8, 8), 8)
            terms = [trade_ref[j, at, k * LANES:(k + 1) * LANES] * ratios[k] for k in range(blocks)]
            total = tree_sum(terms) * spread_ref[at, j * LANES:(j + 1) * LANES]
            total_ref[at, :] = total if j == 0 else total_ref[at, :] + total
            return carry

        lax.fori_loop(0, rows // 8, step, 0, unroll=8)
    for p in range(rows // LANES):
        piece = jnp.sum(jnp.transpose(total_ref[p * LANES:(p + 1) * LANES, :]), axis=0, keepdims=True)
        send_ref[:, p, :] = jnp.broadcast_to(piece, (send_ref.shape[0], LANES))


def settle_kernel(workers_ref, wage_ref, sales_ref, raw_ref, send_ref):
    raw = next_wage(wage_ref, workers_ref, sales_ref)
    raw_ref[...] = raw
    copies = send_ref.shape[0]
    for row, wage in enumerate((raw, wage_ref[...])):
        world = jnp.sum(wage * workers_ref[...], axis=0, keepdims=True)
        send_ref[:, row, :] = jnp.broadcast_to(world, (copies, LANES))


def finish_kernel(cells, raw_ref, price_ref, got_ref, wage_ref, log_price_ref, world_ref):
    sums = jnp.sum(jnp.sum(got_ref[...], axis=0), axis=1, keepdims=True)
    wage_ref[...] = raw_ref[...] * (cells / sums[0:1])
    log_price_ref[...] = price_ref[...] + jnp.log(cells / sums[1:2])
    world_ref[...] = jnp.broadcast_to(sums[0:1], (1, LANES))


VM = pl.BlockSpec(memory_space=pltpu.VMEM)
SM = pl.BlockSpec(memory_space=pltpu.SMEM)


def call(body, out_shape, scalars, arrays, scratch=(), in_place=()):
    return pl.pallas_call(
        body,
        out_shape=tuple(out_shape),
        in_specs=[SM] * len(scalars) + [VM] * len(arrays) + [pl.BlockSpec(memory_space=pl.ANY)] * len(in_place),
        out_specs=(VM,) * len(out_shape),
        scratch_shapes=[pltpu.VMEM(s, jnp.float32) if isinstance(s, tuple) else s for s in scratch],
        compiler_params=pltpu.CompilerParams(vmem_limit_bytes=16 << 20),
    )(*scalars, *arrays, *in_place)


def exchange(x, axis, groups=None):
    return lax.all_to_all(x, axis, 0, 0, tiled=True, axis_index_groups=groups)


def gather(x, axis):
    return exchange(jnp.broadcast_to(x, (lax.axis_size(axis), *x.shape)), axis)


def careful(log_cost, elasticity, productivity, preference, workers, start_wage):
    rows, columns = log_cost.shape
    sectors = elasticity.shape[0]
    across = lax.axis_size("orig")
    cells, width = rows * across, columns // across
    spend_share = preference / jnp.sum(preference, axis=0, keepdims=True)

    def settle(raw_wage, wanted):
        world_income = jnp.sum(gather(jnp.sum(raw_wage * workers, keepdims=True), "orig"))
        wage = raw_wage * (cells / world_income)
        if not wanted:
            return wage, None
        incomes = gather(wage * workers, "orig").reshape(cells)
        return wage, lax.dynamic_slice_in_dim(incomes, lax.axis_index("dest") * columns, columns)

    def kernel_of(slope):
        return jnp.exp(-slope * log_cost.astype(jnp.float32))

    def phi_term(pair):
        return jnp.dot(pair[1], kernel_of(pair[0]), precision=lax.Precision.HIGHEST)

    def sales_term(pair):
        return jnp.dot(kernel_of(pair[0]), pair[1], precision=lax.Precision.HIGHEST)

    def whole(x):
        return jnp.moveaxis(gather(x, "orig"), 0, 1).reshape(sectors, columns)

    wage, dest_income = settle(start_wage, True)
    for step in range(ITERS):
        supply = productivity * jnp.exp(-elasticity[:, None] * jnp.log(wage)[None, :])
        spending = spend_share * dest_income[None, :]
        partial_phi = lax.map(phi_term, (elasticity, supply)).reshape(sectors, across, width)
        phi = whole(jnp.sum(exchange(jnp.moveaxis(partial_phi, 1, 0), "orig"), axis=0))
        log_price = -jnp.log(phi) / elasticity[:, None]
        partial_sales = lax.map(sales_term, (elasticity, spending / phi))
        revenue = jnp.sum(gather(jnp.sum(supply * partial_sales, axis=0), "dest"), axis=0)
        raw_wage = wage * jnp.sqrt(revenue / (wage * workers))
        wage, dest_income = settle(raw_wage, step + 1 < ITERS)
    return wage, log_price


def fast(log_cost, elasticity, productivity, preference, workers, start_wage):
    sectors, rows = productivity.shape
    columns = log_cost.shape[1]
    across, along = lax.axis_size("orig"), lax.axis_size("dest")
    cells = float(rows * across)
    pieces = rows // LANES
    outer = across // INNER
    by_inner = [[i * INNER + j for j in range(INNER)] for i in range(outer)]
    by_outer = [[i * INNER + j for i in range(outer)] for j in range(INNER)]
    workers = workers.reshape(pieces, LANES)
    wage = start_wage.reshape(pieces, LANES)
    sales = trade = None
    for step in range(ITERS):
        last = step + 1 == ITERS
        width = columns + (2 if step == 0 else 1) * LANES
        outs = [f32(outer, sectors, width), f32(rows, sectors * LANES)]
        scratch = [(sectors, 8, columns), (sectors, rows), (sectors, width)]
        if step == 0:
            send, spread, trade, facts = call(
                first_phi_kernel, outs + [f32(sectors, rows, columns), f32(2 * sectors, LANES)], [], [],
                scratch + [pltpu.VMEM(log_cost.shape, log_cost.dtype), pltpu.SMEM((sectors,), jnp.float32)]
                + [(sectors, rows), (pieces, LANES), (pieces, LANES)]
                + [pltpu.SemaphoreType.DMA((2,)), pltpu.SemaphoreType.DMA((4,))],
                [log_cost, elasticity, productivity, workers, wage],
            )
        else:
            send, spread, wage = call(
                functools.partial(phi_kernel, 1.0 if step == 1 else GAIN),
                outs + [f32(pieces, LANES)], [],
                [facts, trade, productivity, workers, wage, sales], scratch,
            )
        got = exchange(send, "orig", by_outer)
        send, = call(sum_kernel, [f32(INNER, sectors, width)], [], [got])
        got = exchange(send, "orig", by_inner)
        made = call(
            functools.partial(sales_kernel, last, cells),
            [f32(along, pieces, LANES)] + ([f32(sectors, columns)] if last else []),
            [],
            [facts, trade, spread, preference, got],
            [(rows, LANES), (sectors, columns), (sectors, width)],
        )
        sales = exchange(made[0], "dest")
    raw, send = call(settle_kernel, [f32(pieces, LANES), f32(across, 2, LANES)], [], [workers, wage, sales])
    got = exchange(send, "orig")
    wage, log_price, world = call(
        functools.partial(finish_kernel, cells),
        [f32(pieces, LANES), f32(sectors, columns), f32(1, LANES)], [], [raw, made[1], got],
    )
    return wage.reshape(rows), log_price, world[0, 0]


def on_device(*args):
    wage, log_price, world = fast(*args)
    return lax.cond(jnp.isfinite(world), lambda: (wage, log_price), lambda: careful(*args))


def solution(mesh):
    return jax.shard_map(
        on_device,
        mesh=mesh,
        in_specs=(P("orig", "dest"), P(), P(None, "orig"), P(None, "dest"), P("orig"), P("orig")),
        out_specs=(P("orig"), P(None, "dest")),
        check_vma=False,
    )
```

```python
import functools

import jax
import jax.numpy as jnp
from jax import lax
from jax.experimental import pallas as pl
from jax.experimental.pallas import tpu as pltpu
from jax.sharding import PartitionSpec as P

ITERS = 3
LANES = 128
CENTRE = 1024.0
GAIN = 2.0
INNER = 8
SMALLEST, LARGEST = 1e-32, 1e30


def f32(*shape):
    return jax.ShapeDtypeStruct(shape, jnp.float32)


def tree_sum(terms):
    while len(terms) > 1:
        terms = [a + b for a, b in zip(terms[::2], terms[1::2])]
    return terms[0]


def pick(vector_ref, count):
    row = lax.broadcasted_iota(jnp.int32, (count, LANES), 0)
    out = jnp.zeros((count, LANES), jnp.float32)
    for j in range(count):
        out = jnp.where(row == j, vector_ref[j], out)
    return out


def total_of(x):
    return jnp.sum(jnp.sum(x, axis=0, keepdims=True), axis=1, keepdims=True)


def next_wage(wage_ref, workers_ref, sales_ref, gain=1.0):
    wage, workers = wage_ref[...], workers_ref[...]
    revenue = jnp.sum(sales_ref[...], axis=0)
    return wage * gain * jnp.sqrt(revenue / (wage * workers))


def supply_of(slopes, productivity_ref, wage):
    log_wage = jnp.log(wage)
    pieces = wage.shape[0]
    return [
        productivity_ref[:, p * LANES:(p + 1) * LANES] * jnp.exp(-slopes * log_wage[p:p + 1])
        for p in range(pieces)
    ]


def spread_over_lanes(supply_ref, spread_ref):
    sectors = supply_ref.shape[0]
    row = lax.broadcasted_iota(jnp.int32, (sectors, sectors * LANES), 0)
    lane = lax.broadcasted_iota(jnp.int32, (sectors, sectors * LANES), 1)
    ones = jnp.where((lane >= row * LANES) & (lane < (row + 1) * LANES), 1.0, 0.0).astype(jnp.bfloat16)
    rest, terms = supply_ref[...], []
    for _ in range(3):
        terms.append(rest.astype(jnp.bfloat16))
        rest = rest - terms[-1].astype(jnp.float32)
    spread_ref[...] = lax.dot_general(
        jnp.concatenate(terms, axis=0), jnp.concatenate([ones] * 3, axis=0), (((0,), (0,)), ((), ())),
        preferred_element_type=jnp.float32,
    )


def prepare(slopes, here, columns, productivity_ref, workers_ref, wage, part_ref, spread_ref, supply_ref):
    sectors, rows = productivity_ref.shape
    pieces = rows // LANES
    supply = supply_of(slopes, productivity_ref, wage)
    for p in range(pieces):
        supply_ref[:, p * LANES:(p + 1) * LANES] = supply[p]
    spread_over_lanes(supply_ref, spread_ref)
    least = functools.reduce(jnp.minimum, supply)
    least = jnp.min(jnp.min(least, axis=0, keepdims=True), axis=1, keepdims=True)
    income = wage * workers_ref[...]
    guarded = jnp.where(least > SMALLEST, income, jnp.nan)
    for i in range(columns // rows):
        part_ref[i * pieces:(i + 1) * pieces, columns:columns + LANES] = guarded * here[i:i + 1]
    if part_ref.shape[1] > columns + LANES:
        part_ref[:, columns + LANES:] = jnp.zeros((sectors, LANES), jnp.float32)
        part_ref[:pieces, columns + LANES:] = income


def send_phi(totals_ref, part_ref, send_ref):
    sectors, _, columns = totals_ref.shape
    for j in range(sectors):
        for k in range(columns // LANES):
            lanes = slice(k * LANES, (k + 1) * LANES)
            part_ref[j:j + 1, lanes] = jnp.sum(totals_ref[j, :, lanes], axis=0, keepdims=True)
    part = part_ref[...]
    for copy in range(send_ref.shape[0]):
        send_ref[copy] = part


def first_phi_kernel(
    cost_in_ref, slope_in_ref, productivity_in_ref, workers_in_ref, wage_in_ref,
    send_ref, spread_ref, trade_ref, facts_ref,
    totals_ref, supply_ref, part_ref, cost_ref, slope_ref, productivity_ref, workers_ref, wage_ref, arrived, brought,
):
    sectors, rows = productivity_ref.shape
    columns = cost_ref.shape[1]
    batch, height = rows // arrived.shape[0], 32
    small = [
        pltpu.make_async_copy(given, held, brought.at[i])
        for i, (given, held) in enumerate(
            ((slope_in_ref, slope_ref), (wage_in_ref, wage_ref), (productivity_in_ref, productivity_ref), (workers_in_ref, workers_ref))
        )
    ]
    copies = []
    for i in range(arrived.shape[0]):
        some = pl.ds(i * batch, batch)
        copies.append(pltpu.make_async_copy(cost_in_ref.at[some], cost_ref.at[some], arrived.at[i]))
    for copy in small + copies:
        copy.start()
    part = lax.axis_index("orig") - lax.axis_index("dest") * (columns // rows)
    row = lax.broadcasted_iota(jnp.int32, (sectors, LANES), 0)
    facts_ref[sectors:, :] = jnp.where(row == part, 1.0, 0.0)
    for copy in small:
        copy.wait()
    facts_ref[:sectors, :] = pick(slope_ref, sectors)
    facts = facts_ref[...]
    prepare(facts[:sectors], facts[sectors:], columns, productivity_ref, workers_ref, wage_ref[...], part_ref, spread_ref, supply_ref)
    slopes = [-slope_ref[j] for j in range(sectors)]
    totals_ref[...] = jnp.zeros_like(totals_ref)

    def step(block, carry):
        at = pl.ds(pl.multiple_of(block * height, height), height)
        for k in range(columns // LANES):
            lanes = slice(k * LANES, (k + 1) * LANES)
            cost = cost_ref[at, lanes].astype(jnp.float32)
            for j in range(sectors):
                trade = jnp.exp(cost * slopes[j])
                trade_ref[j, at, lanes] = trade
                term = trade * spread_ref[at, j * LANES:(j + 1) * LANES]
                totals_ref[j, :, lanes] += tree_sum([term[r:r + 8] for r in range(0, height, 8)])
        return carry

    for i, copy in enumerate(copies):
        copy.wait()
        lax.fori_loop(i * batch // height, (i + 1) * batch // height, step, 0)
    send_phi(totals_ref, part_ref, send_ref)


def phi_kernel(gain, facts_ref, trade_ref, productivity_ref, workers_ref, wage_ref, sales_ref, send_ref, spread_ref, new_wage_ref, totals_ref, supply_ref, part_ref):
    sectors, rows, columns = trade_ref.shape
    blocks = columns // LANES
    wage = next_wage(wage_ref, workers_ref, sales_ref, gain)
    new_wage_ref[...] = wage
    prepare(facts_ref[:sectors], facts_ref[sectors:], columns, productivity_ref, workers_ref, wage, part_ref, spread_ref, supply_ref)
    for j in range(sectors):
        def step(block, totals):
            at = pl.ds(pl.multiple_of(block * 8, 8), 8)
            weight = spread_ref[at, j * LANES:(j + 1) * LANES]
            return tuple(totals[k] + trade_ref[j, at, k * LANES:(k + 1) * LANES] * weight for k in range(blocks))

        zero = jnp.zeros((8, LANES), jnp.float32)
        totals = lax.fori_loop(0, rows // 8, step, (zero,) * blocks, unroll=16)
        for k in range(blocks):
            totals_ref[j, :, k * LANES:(k + 1) * LANES] = totals[k]
    send_phi(totals_ref, part_ref, send_ref)


def sum_kernel(got_ref, send_ref):
    total = jnp.sum(got_ref[...], axis=0)
    for copy in range(send_ref.shape[0]):
        send_ref[copy] = total


def sales_kernel(last, cells, facts_ref, trade_ref, spread_ref, preference_ref, got_ref, send_ref, *rest):
    total_ref, ratio_ref, sums_ref = rest[-3:]
    sectors, rows, columns = trade_ref.shape
    blocks = columns // LANES
    sums_ref[...] = jnp.sum(got_ref[...], axis=0)
    preference = preference_ref[...]
    share = preference / jnp.sum(preference, axis=0, keepdims=True)
    for k in range(blocks):
        lanes = slice(k * LANES, (k + 1) * LANES)
        phi = sums_ref[:, lanes]
        ratio = share[:, lanes] * sums_ref[k:k + 1, columns:columns + LANES] / phi
        ratio_ref[:, lanes] = jnp.where(phi < LARGEST, ratio, jnp.nan)
    if sums_ref.shape[1] > columns + LANES:
        centred = CENTRE * cells / total_of(sums_ref[:, columns + LANES:])
        ratio_ref[...] *= centred * centred
    if last:
        slopes = facts_ref[:sectors]
        for k in range(blocks):
            lanes = slice(k * LANES, (k + 1) * LANES)
            rest[0][:, lanes] = -jnp.log(sums_ref[:, lanes]) / slopes
    for j in range(sectors):
        ratios = [
            jnp.broadcast_to(ratio_ref[j:j + 1, k * LANES:(k + 1) * LANES], (8, LANES))
            for k in range(blocks)
        ]

        def step(block, carry):
            at = pl.ds(pl.multiple_of(block * 8, 8), 8)
            terms = [trade_ref[j, at, k * LANES:(k + 1) * LANES] * ratios[k] for k in range(blocks)]
            total = tree_sum(terms) * spread_ref[at, j * LANES:(j + 1) * LANES]
            total_ref[at, :] = total if j == 0 else total_ref[at, :] + total
            return carry

        lax.fori_loop(0, rows // 8, step, 0, unroll=8)
    for p in range(rows // LANES):
        piece = jnp.sum(jnp.transpose(total_ref[p * LANES:(p + 1) * LANES, :]), axis=0, keepdims=True)
        send_ref[:, p, :] = jnp.broadcast_to(piece, (send_ref.shape[0], LANES))


def settle_kernel(workers_ref, wage_ref, sales_ref, raw_ref, send_ref):
    raw = next_wage(wage_ref, workers_ref, sales_ref)
    raw_ref[...] = raw
    copies = send_ref.shape[0]
    for row, wage in enumerate((raw, wage_ref[...])):
        world = jnp.sum(wage * workers_ref[...], axis=0, keepdims=True)
        send_ref[:, row, :] = jnp.broadcast_to(world, (copies, LANES))


def finish_kernel(cells, raw_ref, price_ref, got_ref, wage_ref, log_price_ref, world_ref):
    sums = jnp.sum(jnp.sum(got_ref[...], axis=0), axis=1, keepdims=True)
    wage_ref[...] = raw_ref[...] * (cells / sums[0:1])
    log_price_ref[...] = price_ref[...] + jnp.log(cells / sums[1:2])
    world_ref[...] = jnp.broadcast_to(sums[0:1], (1, LANES))


VM = pl.BlockSpec(memory_space=pltpu.VMEM)
SM = pl.BlockSpec(memory_space=pltpu.SMEM)


def call(body, out_shape, scalars, arrays, scratch=(), in_place=()):
    return pl.pallas_call(
        body,
        out_shape=tuple(out_shape),
        in_specs=[SM] * len(scalars) + [VM] * len(arrays) + [pl.BlockSpec(memory_space=pl.ANY)] * len(in_place),
        out_specs=(VM,) * len(out_shape),
        scratch_shapes=[pltpu.VMEM(s, jnp.float32) if isinstance(s, tuple) else s for s in scratch],
        compiler_params=pltpu.CompilerParams(vmem_limit_bytes=16 << 20),
    )(*scalars, *arrays, *in_place)


def exchange(x, axis, groups=None):
    return lax.all_to_all(x, axis, 0, 0, tiled=True, axis_index_groups=groups)


def gather(x, axis):
    return exchange(jnp.broadcast_to(x, (lax.axis_size(axis), *x.shape)), axis)


def careful(log_cost, elasticity, productivity, preference, workers, start_wage):
    rows, columns = log_cost.shape
    sectors = elasticity.shape[0]
    across = lax.axis_size("orig")
    cells, width = rows * across, columns // across
    spend_share = preference / jnp.sum(preference, axis=0, keepdims=True)

    def settle(raw_wage, wanted):
        world_income = jnp.sum(gather(jnp.sum(raw_wage * workers, keepdims=True), "orig"))
        wage = raw_wage * (cells / world_income)
        if not wanted:
            return wage, None
        incomes = gather(wage * workers, "orig").reshape(cells)
        return wage, lax.dynamic_slice_in_dim(incomes, lax.axis_index("dest") * columns, columns)

    def kernel_of(slope):
        return jnp.exp(-slope * log_cost.astype(jnp.float32))

    def phi_term(pair):
        return jnp.dot(pair[1], kernel_of(pair[0]), precision=lax.Precision.HIGHEST)

    def sales_term(pair):
        return jnp.dot(kernel_of(pair[0]), pair[1], precision=lax.Precision.HIGHEST)

    def whole(x):
        return jnp.moveaxis(gather(x, "orig"), 0, 1).reshape(sectors, columns)

    wage, dest_income = settle(start_wage, True)
    for step in range(ITERS):
        supply = productivity * jnp.exp(-elasticity[:, None] * jnp.log(wage)[None, :])
        spending = spend_share * dest_income[None, :]
        partial_phi = lax.map(phi_term, (elasticity, supply)).reshape(sectors, across, width)
        phi = whole(jnp.sum(exchange(jnp.moveaxis(partial_phi, 1, 0), "orig"), axis=0))
        log_price = -jnp.log(phi) / elasticity[:, None]
        partial_sales = lax.map(sales_term, (elasticity, spending / phi))
        revenue = jnp.sum(gather(jnp.sum(supply * partial_sales, axis=0), "dest"), axis=0)
        raw_wage = wage * jnp.sqrt(revenue / (wage * workers))
        wage, dest_income = settle(raw_wage, step + 1 < ITERS)
    return wage, log_price


def fast(log_cost, elasticity, productivity, preference, workers, start_wage):
    sectors, rows = productivity.shape
    columns = log_cost.shape[1]
    across, along = lax.axis_size("orig"), lax.axis_size("dest")
    cells = float(rows * across)
    pieces = rows // LANES
    outer = across // INNER
    by_inner = [[i * INNER + j for j in range(INNER)] for i in range(outer)]
    by_outer = [[i * INNER + j for i in range(outer)] for j in range(INNER)]
    workers = workers.reshape(pieces, LANES)
    wage = start_wage.reshape(pieces, LANES)
    sales = trade = None
    for step in range(ITERS):
        last = step + 1 == ITERS
        width = columns + (2 if step == 0 else 1) * LANES
        outs = [f32(outer, sectors, width), f32(rows, sectors * LANES)]
        scratch = [(sectors, 8, columns), (sectors, rows), (sectors, width)]
        if step == 0:
            send, spread, trade, facts = call(
                first_phi_kernel, outs + [f32(sectors, rows, columns), f32(2 * sectors, LANES)], [], [],
                scratch + [pltpu.VMEM(log_cost.shape, log_cost.dtype), pltpu.SMEM((sectors,), jnp.float32)]
                + [(sectors, rows), (pieces, LANES), (pieces, LANES)]
                + [pltpu.SemaphoreType.DMA((2,)), pltpu.SemaphoreType.DMA((4,))],
                [log_cost, elasticity, productivity, workers, wage],
            )
        else:
            send, spread, wage = call(
                functools.partial(phi_kernel, 1.0 if step == 1 else GAIN),
                outs + [f32(pieces, LANES)], [],
                [facts, trade, productivity, workers, wage, sales], scratch,
            )
        got = exchange(send, "orig", by_outer)
        send, = call(sum_kernel, [f32(INNER, sectors, width)], [], [got])
        got = exchange(send, "orig", by_inner)
        made = call(
            functools.partial(sales_kernel, last, cells),
            [f32(along, pieces, LANES)] + ([f32(sectors, columns)] if last else []),
            [],
            [facts, trade, spread, preference, got],
            [(rows, LANES), (sectors, columns), (sectors, width)],
        )
        sales = exchange(made[0], "dest")
    raw, send = call(settle_kernel, [f32(pieces, LANES), f32(across, 2, LANES)], [], [workers, wage, sales])
    got = exchange(send, "orig")
    wage, log_price, world = call(
        functools.partial(finish_kernel, cells),
        [f32(pieces, LANES), f32(sectors, columns), f32(1, LANES)], [], [raw, made[1], got],
    )
    return wage.reshape(rows), log_price, world[0, 0]


def on_device(*args):
    wage, log_price, world = fast(*args)
    done = lax.while_loop(
        lambda state: ~state[2],
        lambda state: (*careful(*args), jnp.bool_(True)),
        (wage, log_price, jnp.isfinite(world)),
    )
    return done[:2]


def solution(mesh):
    return jax.shard_map(
        on_device,
        mesh=mesh,
        in_specs=(P("orig", "dest"), P(), P(None, "orig"), P(None, "dest"), P("orig"), P("orig")),
        out_specs=(P("orig"), P(None, "dest")),
        check_vma=False,
    )
```

```python
import functools

import jax
import jax.numpy as jnp
from jax import lax
from jax.experimental import pallas as pl
from jax.experimental.pallas import tpu as pltpu
from jax.sharding import Mesh
from jax.sharding import PartitionSpec as P

ITERS = 3
LANES = 128
CENTRE = 1024.0
GAIN = 2.0
INNER = 8
ORIG = ("far", "near")
SMALLEST, LARGEST = 1e-32, 1e30


def f32(*shape):
    return jax.ShapeDtypeStruct(shape, jnp.float32)


def tree_sum(terms):
    while len(terms) > 1:
        terms = [a + b for a, b in zip(terms[::2], terms[1::2])]
    return terms[0]


def pick(vector_ref, count):
    row = lax.broadcasted_iota(jnp.int32, (count, LANES), 0)
    out = jnp.zeros((count, LANES), jnp.float32)
    for j in range(count):
        out = jnp.where(row == j, vector_ref[j], out)
    return out


def total_of(x):
    return jnp.sum(jnp.sum(x, axis=0, keepdims=True), axis=1, keepdims=True)


def next_wage(wage_ref, workers_ref, sales_ref, gain=1.0):
    wage, workers = wage_ref[...], workers_ref[...]
    revenue = jnp.sum(sales_ref[...], axis=0)
    return wage * gain * jnp.sqrt(revenue / (wage * workers))


def supply_of(slopes, productivity_ref, wage):
    log_wage = jnp.log(wage)
    pieces = wage.shape[0]
    return [
        productivity_ref[:, p * LANES:(p + 1) * LANES] * jnp.exp(-slopes * log_wage[p:p + 1])
        for p in range(pieces)
    ]


def spread_over_lanes(supply_ref, spread_ref):
    sectors = supply_ref.shape[0]
    row = lax.broadcasted_iota(jnp.int32, (sectors, sectors * LANES), 0)
    lane = lax.broadcasted_iota(jnp.int32, (sectors, sectors * LANES), 1)
    ones = jnp.where((lane >= row * LANES) & (lane < (row + 1) * LANES), 1.0, 0.0).astype(jnp.bfloat16)
    rest, terms = supply_ref[...], []
    for _ in range(3):
        terms.append(rest.astype(jnp.bfloat16))
        rest = rest - terms[-1].astype(jnp.float32)
    spread_ref[...] = lax.dot_general(
        jnp.concatenate(terms, axis=0), jnp.concatenate([ones] * 3, axis=0), (((0,), (0,)), ((), ())),
        preferred_element_type=jnp.float32,
    )


def prepare(slopes, here, columns, productivity_ref, workers_ref, wage, part_ref, spread_ref, supply_ref):
    sectors, rows = productivity_ref.shape
    pieces = rows // LANES
    supply = supply_of(slopes, productivity_ref, wage)
    for p in range(pieces):
        supply_ref[:, p * LANES:(p + 1) * LANES] = supply[p]
    spread_over_lanes(supply_ref, spread_ref)
    least = functools.reduce(jnp.minimum, supply)
    least = jnp.min(jnp.min(least, axis=0, keepdims=True), axis=1, keepdims=True)
    income = wage * workers_ref[...]
    guarded = jnp.where(least > SMALLEST, income, jnp.nan)
    for i in range(columns // rows):
        part_ref[i * pieces:(i + 1) * pieces, columns:columns + LANES] = guarded * here[i:i + 1]
    if part_ref.shape[1] > columns + LANES:
        part_ref[:, columns + LANES:] = jnp.zeros((sectors, LANES), jnp.float32)
        part_ref[:pieces, columns + LANES:] = income


def send_phi(totals_ref, part_ref, send_ref):
    sectors, _, columns = totals_ref.shape
    for j in range(sectors):
        for k in range(columns // LANES):
            lanes = slice(k * LANES, (k + 1) * LANES)
            part_ref[j:j + 1, lanes] = jnp.sum(totals_ref[j, :, lanes], axis=0, keepdims=True)
    part = part_ref[...]
    for copy in range(send_ref.shape[0]):
        send_ref[copy] = part


def first_phi_kernel(
    cost_in_ref, slope_in_ref, productivity_in_ref, workers_in_ref, wage_in_ref,
    send_ref, spread_ref, trade_ref, facts_ref,
    totals_ref, supply_ref, part_ref, cost_ref, slope_ref, productivity_ref, workers_ref, wage_ref, arrived, brought,
):
    sectors, rows = productivity_ref.shape
    columns = cost_ref.shape[1]
    batch, height = rows // arrived.shape[0], 32
    small = [
        pltpu.make_async_copy(given, held, brought.at[i])
        for i, (given, held) in enumerate(
            ((slope_in_ref, slope_ref), (wage_in_ref, wage_ref), (productivity_in_ref, productivity_ref), (workers_in_ref, workers_ref))
        )
    ]
    copies = []
    for i in range(arrived.shape[0]):
        some = pl.ds(i * batch, batch)
        copies.append(pltpu.make_async_copy(cost_in_ref.at[some], cost_ref.at[some], arrived.at[i]))
    for copy in small + copies:
        copy.start()
    part = lax.axis_index("far") * INNER + lax.axis_index("near") - lax.axis_index("dest") * (columns // rows)
    row = lax.broadcasted_iota(jnp.int32, (sectors, LANES), 0)
    facts_ref[sectors:, :] = jnp.where(row == part, 1.0, 0.0)
    for copy in small:
        copy.wait()
    facts_ref[:sectors, :] = pick(slope_ref, sectors)
    facts = facts_ref[...]
    prepare(facts[:sectors], facts[sectors:], columns, productivity_ref, workers_ref, wage_ref[...], part_ref, spread_ref, supply_ref)
    slopes = [-slope_ref[j] for j in range(sectors)]
    totals_ref[...] = jnp.zeros_like(totals_ref)

    def step(block, carry):
        at = pl.ds(pl.multiple_of(block * height, height), height)
        for k in range(columns // LANES):
            lanes = slice(k * LANES, (k + 1) * LANES)
            cost = cost_ref[at, lanes].astype(jnp.float32)
            for j in range(sectors):
                trade = jnp.exp(cost * slopes[j])
                trade_ref[j, at, lanes] = trade
                term = trade * spread_ref[at, j * LANES:(j + 1) * LANES]
                totals_ref[j, :, lanes] += tree_sum([term[r:r + 8] for r in range(0, height, 8)])
        return carry

    for i, copy in enumerate(copies):
        copy.wait()
        lax.fori_loop(i * batch // height, (i + 1) * batch // height, step, 0)
    send_phi(totals_ref, part_ref, send_ref)


def phi_kernel(gain, facts_ref, trade_ref, productivity_ref, workers_ref, wage_ref, sales_ref, send_ref, spread_ref, new_wage_ref, totals_ref, supply_ref, part_ref):
    sectors, rows, columns = trade_ref.shape
    blocks = columns // LANES
    wage = next_wage(wage_ref, workers_ref, sales_ref, gain)
    new_wage_ref[...] = wage
    prepare(facts_ref[:sectors], facts_ref[sectors:], columns, productivity_ref, workers_ref, wage, part_ref, spread_ref, supply_ref)
    for j in range(sectors):
        def step(block, totals):
            at = pl.ds(pl.multiple_of(block * 8, 8), 8)
            weight = spread_ref[at, j * LANES:(j + 1) * LANES]
            return tuple(totals[k] + trade_ref[j, at, k * LANES:(k + 1) * LANES] * weight for k in range(blocks))

        zero = jnp.zeros((8, LANES), jnp.float32)
        totals = lax.fori_loop(0, rows // 8, step, (zero,) * blocks, unroll=16)
        for k in range(blocks):
            totals_ref[j, :, k * LANES:(k + 1) * LANES] = totals[k]
    send_phi(totals_ref, part_ref, send_ref)


def sum_kernel(got_ref, send_ref, *rest):
    width = send_ref.shape[2]
    total = jnp.sum(got_ref[:, :, :width], axis=0)
    for copy in range(send_ref.shape[0]):
        send_ref[copy] = total
    for incomes_ref in rest:
        incomes_ref[...] = got_ref[:, :incomes_ref.shape[1], width:]


def sales_kernel(last, cells, facts_ref, trade_ref, spread_ref, preference_ref, got_ref, send_ref, *rest):
    total_ref, ratio_ref, sums_ref = rest[-3:]
    sectors, rows, columns = trade_ref.shape
    blocks = columns // LANES
    sums_ref[...] = jnp.sum(got_ref[...], axis=0)
    preference = preference_ref[...]
    share = preference / jnp.sum(preference, axis=0, keepdims=True)
    for k in range(blocks):
        lanes = slice(k * LANES, (k + 1) * LANES)
        phi = sums_ref[:, lanes]
        ratio = share[:, lanes] * sums_ref[k:k + 1, columns:columns + LANES] / phi
        ratio_ref[:, lanes] = jnp.where(phi < LARGEST, ratio, jnp.nan)
    if sums_ref.shape[1] > columns + LANES:
        centred = CENTRE * cells / total_of(sums_ref[:, columns + LANES:])
        ratio_ref[...] *= centred * centred
    if last:
        slopes = facts_ref[:sectors]
        for k in range(blocks):
            lanes = slice(k * LANES, (k + 1) * LANES)
            rest[0][:, lanes] = -jnp.log(sums_ref[:, lanes]) / slopes
    for j in range(sectors):
        ratios = [
            jnp.broadcast_to(ratio_ref[j:j + 1, k * LANES:(k + 1) * LANES], (8, LANES))
            for k in range(blocks)
        ]

        def step(block, carry):
            at = pl.ds(pl.multiple_of(block * 8, 8), 8)
            terms = [trade_ref[j, at, k * LANES:(k + 1) * LANES] * ratios[k] for k in range(blocks)]
            total = tree_sum(terms) * spread_ref[at, j * LANES:(j + 1) * LANES]
            total_ref[at, :] = total if j == 0 else total_ref[at, :] + total
            return carry

        lax.fori_loop(0, rows // 8, step, 0, unroll=8)
    for p in range(rows // LANES):
        piece = jnp.sum(jnp.transpose(total_ref[p * LANES:(p + 1) * LANES, :]), axis=0, keepdims=True)
        send_ref[:, p, :] = jnp.broadcast_to(piece, (send_ref.shape[0], LANES))


def settle_kernel(incomes_ref, wage_ref, sales_ref, raw_ref, send_ref):
    far = incomes_ref.shape[0]
    along = sales_ref.shape[0] // far
    mine = lax.axis_index("far")
    world = jnp.zeros((1, LANES), jnp.float32)
    for i in range(far):
        income = incomes_ref[i]
        grown = jnp.sqrt(jnp.sum(sales_ref[i * along:(i + 1) * along], axis=0) / income)
        world += jnp.sum(income * grown, axis=0, keepdims=True)

        @pl.when(mine == i)
        def _():
            raw_ref[...] = wage_ref[...] * grown

    before = jnp.sum(jnp.sum(incomes_ref[...], axis=0), axis=0, keepdims=True)
    for row, sums in enumerate((world, before)):
        send_ref[:, row, :] = jnp.broadcast_to(sums, (send_ref.shape[0], LANES))


def finish_kernel(cells, raw_ref, price_ref, got_ref, wage_ref, log_price_ref, world_ref):
    sums = jnp.sum(jnp.sum(got_ref[...], axis=0), axis=1, keepdims=True)
    wage_ref[...] = raw_ref[...] * (cells / sums[0:1])
    log_price_ref[...] = price_ref[...] + jnp.log(cells / sums[1:2])
    world_ref[...] = jnp.broadcast_to(sums[0:1], (1, LANES))


VM = pl.BlockSpec(memory_space=pltpu.VMEM)
SM = pl.BlockSpec(memory_space=pltpu.SMEM)


def call(body, out_shape, scalars, arrays, scratch=(), in_place=()):
    return pl.pallas_call(
        body,
        out_shape=tuple(out_shape),
        in_specs=[SM] * len(scalars) + [VM] * len(arrays) + [pl.BlockSpec(memory_space=pl.ANY)] * len(in_place),
        out_specs=(VM,) * len(out_shape),
        scratch_shapes=[pltpu.VMEM(s, jnp.float32) if isinstance(s, tuple) else s for s in scratch],
        compiler_params=pltpu.CompilerParams(vmem_limit_bytes=16 << 20),
    )(*scalars, *arrays, *in_place)


def exchange(x, axis):
    return lax.all_to_all(x, axis, 0, 0, tiled=True)


def gather(x, axis):
    return exchange(jnp.broadcast_to(x, (lax.axis_size(axis), *x.shape)), axis)


def careful(log_cost, elasticity, productivity, preference, workers, start_wage):
    rows, columns = log_cost.shape
    sectors = elasticity.shape[0]
    across = lax.axis_size(ORIG)
    cells, width = rows * across, columns // across
    spend_share = preference / jnp.sum(preference, axis=0, keepdims=True)

    def settle(raw_wage, wanted):
        world_income = jnp.sum(gather(jnp.sum(raw_wage * workers, keepdims=True), ORIG))
        wage = raw_wage * (cells / world_income)
        if not wanted:
            return wage, None
        incomes = gather(wage * workers, ORIG).reshape(cells)
        return wage, lax.dynamic_slice_in_dim(incomes, lax.axis_index("dest") * columns, columns)

    def kernel_of(slope):
        return jnp.exp(-slope * log_cost.astype(jnp.float32))

    def phi_term(pair):
        return jnp.dot(pair[1], kernel_of(pair[0]), precision=lax.Precision.HIGHEST)

    def sales_term(pair):
        return jnp.dot(kernel_of(pair[0]), pair[1], precision=lax.Precision.HIGHEST)

    def whole(x):
        return jnp.moveaxis(gather(x, ORIG), 0, 1).reshape(sectors, columns)

    wage, dest_income = settle(start_wage, True)
    for step in range(ITERS):
        supply = productivity * jnp.exp(-elasticity[:, None] * jnp.log(wage)[None, :])
        spending = spend_share * dest_income[None, :]
        partial_phi = lax.map(phi_term, (elasticity, supply)).reshape(sectors, across, width)
        phi = whole(jnp.sum(exchange(jnp.moveaxis(partial_phi, 1, 0), ORIG), axis=0))
        log_price = -jnp.log(phi) / elasticity[:, None]
        partial_sales = lax.map(sales_term, (elasticity, spending / phi))
        revenue = jnp.sum(gather(jnp.sum(supply * partial_sales, axis=0), "dest"), axis=0)
        raw_wage = wage * jnp.sqrt(revenue / (wage * workers))
        wage, dest_income = settle(raw_wage, step + 1 < ITERS)
    return wage, log_price


def fast(log_cost, elasticity, productivity, preference, workers, start_wage):
    sectors, rows = productivity.shape
    columns = log_cost.shape[1]
    outer, along = lax.axis_size("far"), lax.axis_size("dest")
    cells = float(rows * outer * INNER)
    pieces = rows // LANES
    workers = workers.reshape(pieces, LANES)
    wage = start_wage.reshape(pieces, LANES)
    sales = trade = None
    for step in range(ITERS):
        last = step + 1 == ITERS
        width = columns + (1 if step == 1 else 2) * LANES
        summed = columns + (2 if step == 0 else 1) * LANES
        outs = [f32(outer, sectors, width), f32(rows, sectors * LANES)]
        scratch = [(sectors, 8, columns), (sectors, rows), (sectors, width)]
        if step == 0:
            send, spread, trade, facts = call(
                first_phi_kernel, outs + [f32(sectors, rows, columns), f32(2 * sectors, LANES)], [], [],
                scratch + [pltpu.VMEM(log_cost.shape, log_cost.dtype), pltpu.SMEM((sectors,), jnp.float32)]
                + [(sectors, rows), (pieces, LANES), (pieces, LANES)]
                + [pltpu.SemaphoreType.DMA((2,)), pltpu.SemaphoreType.DMA((4,))],
                [log_cost, elasticity, productivity, workers, wage],
            )
        else:
            send, spread, wage = call(
                functools.partial(phi_kernel, 1.0 if step == 1 else GAIN),
                outs + [f32(pieces, LANES)], [],
                [facts, trade, productivity, workers, wage, sales], scratch,
            )
        got = exchange(send, "far")
        send, *incomes = call(
            sum_kernel, [f32(INNER, sectors, summed)] + ([f32(outer, pieces, LANES)] if last else []), [], [got]
        )
        got = exchange(send, "near")
        made = call(
            functools.partial(sales_kernel, last, cells),
            [f32(outer * along if last else along, pieces, LANES)] + ([f32(sectors, columns)] if last else []),
            [],
            [facts, trade, spread, preference, got],
            [(rows, LANES), (sectors, columns), (sectors, summed)],
        )
        sales = exchange(made[0], ("far", "dest") if last else "dest")
    raw, send = call(settle_kernel, [f32(pieces, LANES), f32(INNER, 2, LANES)], [], [*incomes, wage, sales])
    got = exchange(send, "near")
    wage, log_price, world = call(
        functools.partial(finish_kernel, cells),
        [f32(pieces, LANES), f32(sectors, columns), f32(1, LANES)], [], [raw, made[1], got],
    )
    return wage.reshape(rows), log_price, world[0, 0]


def on_device(*args):
    wage, log_price, world = fast(*args)
    done = lax.while_loop(
        lambda state: ~state[2],
        lambda state: (*careful(*args), jnp.bool_(True)),
        (wage, log_price, jnp.isfinite(world)),
    )
    return done[:2]


def solution(mesh):
    across, along = mesh.devices.shape
    split = Mesh(mesh.devices.reshape(across // INNER, INNER, along), (*ORIG, "dest"))
    return jax.shard_map(
        on_device,
        mesh=split,
        in_specs=(P(ORIG, "dest"), P(), P(None, ORIG), P(None, "dest"), P(ORIG), P(ORIG)),
        out_specs=(P(ORIG), P(None, "dest")),
        check_vma=False,
    )
```

```python
import functools

import jax
import jax.numpy as jnp
from jax import lax
from jax.experimental import pallas as pl
from jax.experimental.pallas import tpu as pltpu
from jax.sharding import Mesh
from jax.sharding import PartitionSpec as P

ITERS = 3
LANES = 128
CENTRE = 1024.0
GAIN = 2.0
INNER = 8
ORIG = ("far", "near")
SMALLEST, LARGEST = 1e-32, 1e30


def f32(*shape):
    return jax.ShapeDtypeStruct(shape, jnp.float32)


def tree_sum(terms):
    while len(terms) > 1:
        terms = [a + b for a, b in zip(terms[::2], terms[1::2])]
    return terms[0]


def pick(vector_ref, count):
    row = lax.broadcasted_iota(jnp.int32, (count, LANES), 0)
    out = jnp.zeros((count, LANES), jnp.float32)
    for j in range(count):
        out = jnp.where(row == j, vector_ref[j], out)
    return out


def total_of(x):
    return jnp.sum(jnp.sum(x, axis=0, keepdims=True), axis=1, keepdims=True)


def next_wage(wage_ref, workers_ref, sales_ref, gain=1.0):
    wage, workers = wage_ref[...], workers_ref[...]
    revenue = jnp.sum(sales_ref[...], axis=0)
    return wage * gain * jnp.sqrt(revenue / (wage * workers))


def supply_of(slopes, productivity_ref, wage):
    log_wage = jnp.log(wage)
    pieces = wage.shape[0]
    return [
        productivity_ref[:, p * LANES:(p + 1) * LANES] * jnp.exp(-slopes * log_wage[p:p + 1])
        for p in range(pieces)
    ]


def spread_over_lanes(supply_ref, spread_ref):
    sectors = supply_ref.shape[0]
    row = lax.broadcasted_iota(jnp.int32, (sectors, sectors * LANES), 0)
    lane = lax.broadcasted_iota(jnp.int32, (sectors, sectors * LANES), 1)
    ones = jnp.where((lane >= row * LANES) & (lane < (row + 1) * LANES), 1.0, 0.0).astype(jnp.bfloat16)
    rest, terms = supply_ref[...], []
    for _ in range(3):
        terms.append(rest.astype(jnp.bfloat16))
        rest = rest - terms[-1].astype(jnp.float32)
    spread_ref[...] = lax.dot_general(
        jnp.concatenate(terms, axis=0), jnp.concatenate([ones] * 3, axis=0), (((0,), (0,)), ((), ())),
        preferred_element_type=jnp.float32,
    )


def prepare(slopes, here, columns, productivity_ref, workers_ref, wage, part_ref, spread_ref, supply_ref):
    sectors, rows = productivity_ref.shape
    pieces = rows // LANES
    supply = supply_of(slopes, productivity_ref, wage)
    for p in range(pieces):
        supply_ref[:, p * LANES:(p + 1) * LANES] = supply[p]
    spread_over_lanes(supply_ref, spread_ref)
    least = functools.reduce(jnp.minimum, supply)
    least = jnp.min(jnp.min(least, axis=0, keepdims=True), axis=1, keepdims=True)
    income = wage * workers_ref[...]
    guarded = jnp.where(least > SMALLEST, income, jnp.nan)
    for i in range(columns // rows):
        part_ref[i * pieces:(i + 1) * pieces, columns:columns + LANES] = guarded * here[i:i + 1]
    if part_ref.shape[1] > columns + LANES:
        part_ref[:, columns + LANES:] = jnp.zeros((sectors, LANES), jnp.float32)
        part_ref[:pieces, columns + LANES:] = income


def send_phi(totals_ref, part_ref, send_ref):
    sectors, _, columns = totals_ref.shape
    for j in range(sectors):
        for k in range(columns // LANES):
            lanes = slice(k * LANES, (k + 1) * LANES)
            part_ref[j:j + 1, lanes] = jnp.sum(totals_ref[j, :, lanes], axis=0, keepdims=True)
    part = part_ref[...]
    for copy in range(send_ref.shape[0]):
        send_ref[copy] = part


def first_phi_kernel(
    cost_in_ref, slope_in_ref, productivity_in_ref, workers_in_ref, wage_in_ref,
    send_ref, spread_ref, trade_ref, facts_ref,
    totals_ref, supply_ref, part_ref, cost_ref, slope_ref, productivity_ref, workers_ref, wage_ref, arrived, brought,
):
    sectors, rows = productivity_ref.shape
    columns = cost_ref.shape[1]
    batch, height = rows // arrived.shape[0], 32
    small = [
        pltpu.make_async_copy(given, held, brought.at[i])
        for i, (given, held) in enumerate(
            ((slope_in_ref, slope_ref), (wage_in_ref, wage_ref), (productivity_in_ref, productivity_ref), (workers_in_ref, workers_ref))
        )
    ]
    copies = []
    for i in range(arrived.shape[0]):
        some = pl.ds(i * batch, batch)
        copies.append(pltpu.make_async_copy(cost_in_ref.at[some], cost_ref.at[some], arrived.at[i]))
    for copy in small + copies:
        copy.start()
    part = lax.axis_index("far") * INNER + lax.axis_index("near") - lax.axis_index("dest") * (columns // rows)
    row = lax.broadcasted_iota(jnp.int32, (sectors, LANES), 0)
    facts_ref[sectors:, :] = jnp.where(row == part, 1.0, 0.0)
    for copy in small:
        copy.wait()
    facts_ref[:sectors, :] = pick(slope_ref, sectors)
    facts = facts_ref[...]
    prepare(facts[:sectors], facts[sectors:], columns, productivity_ref, workers_ref, wage_ref[...], part_ref, spread_ref, supply_ref)
    slopes = [-slope_ref[j] for j in range(sectors)]
    totals_ref[...] = jnp.zeros_like(totals_ref)

    def step(block, carry):
        at = pl.ds(pl.multiple_of(block * height, height), height)
        for k in range(columns // LANES):
            lanes = slice(k * LANES, (k + 1) * LANES)
            cost = cost_ref[at, lanes].astype(jnp.float32)
            for j in range(sectors):
                trade = jnp.exp(cost * slopes[j])
                trade_ref[j, at, lanes] = trade
                term = trade * spread_ref[at, j * LANES:(j + 1) * LANES]
                totals_ref[j, :, lanes] += tree_sum([term[r:r + 8] for r in range(0, height, 8)])
        return carry

    for i, copy in enumerate(copies):
        copy.wait()
        lax.fori_loop(i * batch // height, (i + 1) * batch // height, step, 0)
    send_phi(totals_ref, part_ref, send_ref)


def phi_kernel(gain, facts_ref, trade_ref, productivity_ref, workers_ref, wage_ref, sales_ref, send_ref, spread_ref, new_wage_ref, totals_ref, supply_ref, part_ref):
    sectors, rows, columns = trade_ref.shape
    blocks = columns // LANES
    wage = next_wage(wage_ref, workers_ref, sales_ref, gain)
    new_wage_ref[...] = wage
    prepare(facts_ref[:sectors], facts_ref[sectors:], columns, productivity_ref, workers_ref, wage, part_ref, spread_ref, supply_ref)
    for j in range(sectors):
        def step(block, totals):
            at = pl.ds(pl.multiple_of(block * 8, 8), 8)
            weight = spread_ref[at, j * LANES:(j + 1) * LANES]
            return tuple(totals[k] + trade_ref[j, at, k * LANES:(k + 1) * LANES] * weight for k in range(blocks))

        zero = jnp.zeros((8, LANES), jnp.float32)
        totals = lax.fori_loop(0, rows // 8, step, (zero,) * blocks, unroll=64)
        for k in range(blocks):
            totals_ref[j, :, k * LANES:(k + 1) * LANES] = totals[k]
    send_phi(totals_ref, part_ref, send_ref)


def sum_kernel(got_ref, send_ref):
    total = jnp.sum(got_ref[...], axis=0)
    for copy in range(send_ref.shape[0]):
        send_ref[copy] = total


def sales_kernel(last, cells, facts_ref, trade_ref, spread_ref, preference_ref, got_ref, send_ref, *rest):
    total_ref, ratio_ref, sums_ref = rest[-3:]
    sectors, rows, columns = trade_ref.shape
    blocks = columns // LANES
    sums_ref[...] = jnp.sum(got_ref[...], axis=0)
    preference = preference_ref[...]
    share = preference / jnp.sum(preference, axis=0, keepdims=True)
    for k in range(blocks):
        lanes = slice(k * LANES, (k + 1) * LANES)
        phi = sums_ref[:, lanes]
        ratio = share[:, lanes] * sums_ref[k:k + 1, columns:columns + LANES] / phi
        ratio_ref[:, lanes] = jnp.where(phi < LARGEST, ratio, jnp.nan)
    if sums_ref.shape[1] > columns + LANES:
        centred = CENTRE * cells / total_of(sums_ref[:, columns + LANES:])
        ratio_ref[...] *= centred * centred
    if last:
        slopes = facts_ref[:sectors]
        for k in range(blocks):
            lanes = slice(k * LANES, (k + 1) * LANES)
            rest[0][:, lanes] = -jnp.log(sums_ref[:, lanes]) / slopes
    for j in range(sectors):
        ratios = [
            jnp.broadcast_to(ratio_ref[j:j + 1, k * LANES:(k + 1) * LANES], (8, LANES))
            for k in range(blocks)
        ]

        def step(block, carry):
            at = pl.ds(pl.multiple_of(block * 8, 8), 8)
            terms = [trade_ref[j, at, k * LANES:(k + 1) * LANES] * ratios[k] for k in range(blocks)]
            total = tree_sum(terms) * spread_ref[at, j * LANES:(j + 1) * LANES]
            total_ref[at, :] = total if j == 0 else total_ref[at, :] + total
            return carry

        lax.fori_loop(0, rows // 8, step, 0, unroll=32)
    for p in range(rows // LANES):
        piece = jnp.sum(jnp.transpose(total_ref[p * LANES:(p + 1) * LANES, :]), axis=0, keepdims=True)
        send_ref[:, p, :] = jnp.broadcast_to(piece, (send_ref.shape[0], LANES))


def settle_kernel(workers_ref, wage_ref, sales_ref, raw_ref, send_ref):
    raw = next_wage(wage_ref, workers_ref, sales_ref)
    raw_ref[...] = raw
    for row, wage in enumerate((raw, wage_ref[...])):
        world = jnp.sum(wage * workers_ref[...], axis=0, keepdims=True)
        send_ref[:, row, :] = jnp.broadcast_to(world, (send_ref.shape[0], LANES))


def finish_kernel(cells, raw_ref, price_ref, got_ref, wage_ref, log_price_ref, world_ref):
    sums = jnp.sum(jnp.sum(got_ref[...], axis=0), axis=1, keepdims=True)
    wage_ref[...] = raw_ref[...] * (cells / sums[0:1])
    log_price_ref[...] = price_ref[...] + jnp.log(cells / sums[1:2])
    world_ref[...] = jnp.broadcast_to(sums[0:1], (1, LANES))


VM = pl.BlockSpec(memory_space=pltpu.VMEM)
SM = pl.BlockSpec(memory_space=pltpu.SMEM)


def call(body, out_shape, scalars, arrays, scratch=(), in_place=()):
    return pl.pallas_call(
        body,
        out_shape=tuple(out_shape),
        in_specs=[SM] * len(scalars) + [VM] * len(arrays) + [pl.BlockSpec(memory_space=pl.ANY)] * len(in_place),
        out_specs=(VM,) * len(out_shape),
        scratch_shapes=[pltpu.VMEM(s, jnp.float32) if isinstance(s, tuple) else s for s in scratch],
        compiler_params=pltpu.CompilerParams(vmem_limit_bytes=16 << 20),
    )(*scalars, *arrays, *in_place)


def exchange(x, axis):
    return lax.all_to_all(x, axis, 0, 0, tiled=True)


def gather(x, axis):
    return exchange(jnp.broadcast_to(x, (lax.axis_size(axis), *x.shape)), axis)


def careful(log_cost, elasticity, productivity, preference, workers, start_wage):
    rows, columns = log_cost.shape
    sectors = elasticity.shape[0]
    across = lax.axis_size(ORIG)
    cells, width = rows * across, columns // across
    spend_share = preference / jnp.sum(preference, axis=0, keepdims=True)

    def settle(raw_wage, wanted):
        world_income = jnp.sum(gather(jnp.sum(raw_wage * workers, keepdims=True), ORIG))
        wage = raw_wage * (cells / world_income)
        if not wanted:
            return wage, None
        incomes = gather(wage * workers, ORIG).reshape(cells)
        return wage, lax.dynamic_slice_in_dim(incomes, lax.axis_index("dest") * columns, columns)

    def kernel_of(slope):
        return jnp.exp(-slope * log_cost.astype(jnp.float32))

    def phi_term(pair):
        return jnp.dot(pair[1], kernel_of(pair[0]), precision=lax.Precision.HIGHEST)

    def sales_term(pair):
        return jnp.dot(kernel_of(pair[0]), pair[1], precision=lax.Precision.HIGHEST)

    def whole(x):
        return jnp.moveaxis(gather(x, ORIG), 0, 1).reshape(sectors, columns)

    wage, dest_income = settle(start_wage, True)
    for step in range(ITERS):
        supply = productivity * jnp.exp(-elasticity[:, None] * jnp.log(wage)[None, :])
        spending = spend_share * dest_income[None, :]
        partial_phi = lax.map(phi_term, (elasticity, supply)).reshape(sectors, across, width)
        phi = whole(jnp.sum(exchange(jnp.moveaxis(partial_phi, 1, 0), ORIG), axis=0))
        log_price = -jnp.log(phi) / elasticity[:, None]
        partial_sales = lax.map(sales_term, (elasticity, spending / phi))
        revenue = jnp.sum(gather(jnp.sum(supply * partial_sales, axis=0), "dest"), axis=0)
        raw_wage = wage * jnp.sqrt(revenue / (wage * workers))
        wage, dest_income = settle(raw_wage, step + 1 < ITERS)
    return wage, log_price


def fast(log_cost, elasticity, productivity, preference, workers, start_wage):
    sectors, rows = productivity.shape
    columns = log_cost.shape[1]
    outer, along = lax.axis_size("far"), lax.axis_size("dest")
    cells = float(rows * outer * INNER)
    pieces = rows // LANES
    workers = workers.reshape(pieces, LANES)
    wage = start_wage.reshape(pieces, LANES)
    sales = trade = None
    for step in range(ITERS):
        last = step + 1 == ITERS
        width = columns + (2 if step == 0 else 1) * LANES
        outs = [f32(outer, sectors, width), f32(rows, sectors * LANES)]
        scratch = [(sectors, 8, columns), (sectors, rows), (sectors, width)]
        if step == 0:
            send, spread, trade, facts = call(
                first_phi_kernel, outs + [f32(sectors, rows, columns), f32(2 * sectors, LANES)], [], [],
                scratch + [pltpu.VMEM(log_cost.shape, log_cost.dtype), pltpu.SMEM((sectors,), jnp.float32)]
                + [(sectors, rows), (pieces, LANES), (pieces, LANES)]
                + [pltpu.SemaphoreType.DMA((2,)), pltpu.SemaphoreType.DMA((4,))],
                [log_cost, elasticity, productivity, workers, wage],
            )
        else:
            send, spread, wage = call(
                functools.partial(phi_kernel, 1.0 if step == 1 else GAIN),
                outs + [f32(pieces, LANES)], [],
                [facts, trade, productivity, workers, wage, sales], scratch,
            )
        got = exchange(send, "far")
        send, = call(sum_kernel, [f32(INNER, sectors, width)], [], [got])
        got = exchange(send, "near")
        made = call(
            functools.partial(sales_kernel, last, cells),
            [f32(along, pieces, LANES)] + ([f32(sectors, columns)] if last else []),
            [],
            [facts, trade, spread, preference, got],
            [(rows, LANES), (sectors, columns), (sectors, width)],
        )
        sales = exchange(made[0], "dest")
    raw, send = call(settle_kernel, [f32(pieces, LANES), f32(outer * INNER, 2, LANES)], [], [workers, wage, sales])
    got = exchange(send, ORIG)
    wage, log_price, world = call(
        functools.partial(finish_kernel, cells),
        [f32(pieces, LANES), f32(sectors, columns), f32(1, LANES)], [], [raw, made[1], got],
    )
    return wage.reshape(rows), log_price, world[0, 0]


def on_device(*args):
    wage, log_price, world = fast(*args)
    done = lax.while_loop(
        lambda state: ~state[2],
        lambda state: (*careful(*args), jnp.bool_(True)),
        (wage, log_price, jnp.isfinite(world)),
    )
    return done[:2]


def solution(mesh):
    across, along = mesh.devices.shape
    split = Mesh(mesh.devices.reshape(across // INNER, INNER, along), (*ORIG, "dest"))
    return jax.shard_map(
        on_device,
        mesh=split,
        in_specs=(P(ORIG, "dest"), P(), P(None, ORIG), P(None, "dest"), P(ORIG), P(ORIG)),
        out_specs=(P(ORIG), P(None, "dest")),
        check_vma=False,
    )
```

```python
import functools

import jax
import jax.numpy as jnp
from jax import lax
from jax.experimental import pallas as pl
from jax.experimental.pallas import tpu as pltpu
from jax.sharding import Mesh
from jax.sharding import PartitionSpec as P

ITERS = 3
LANES = 128
GAINS = (64.0, 4.0)
SMALLEST, LARGEST = 1e-32, 1e30
INNER = 8
ORIG = ("far", "near")
SMALLEST, LARGEST = 1e-32, 1e30


def f32(*shape):
    return jax.ShapeDtypeStruct(shape, jnp.float32)


def tree_sum(terms):
    while len(terms) > 1:
        terms = [a + b for a, b in zip(terms[::2], terms[1::2])]
    return terms[0]


def pick(vector_ref, count):
    row = lax.broadcasted_iota(jnp.int32, (count, LANES), 0)
    out = jnp.zeros((count, LANES), jnp.float32)
    for j in range(count):
        out = jnp.where(row == j, vector_ref[j], out)
    return out


def next_wage(wage_ref, workers_ref, sales_ref, gain=1.0):
    wage, workers = wage_ref[...], workers_ref[...]
    revenue = jnp.sum(sales_ref[...], axis=0)
    return wage * gain * jnp.sqrt(revenue / (wage * workers))


def supply_of(slopes, productivity_ref, wage):
    log_wage = jnp.log(wage)
    pieces = wage.shape[0]
    return [
        productivity_ref[:, p * LANES:(p + 1) * LANES] * jnp.exp(-slopes * log_wage[p:p + 1])
        for p in range(pieces)
    ]


def spread_over_lanes(supply_ref, spread_ref):
    sectors = supply_ref.shape[0]
    row = lax.broadcasted_iota(jnp.int32, (sectors, sectors * LANES), 0)
    lane = lax.broadcasted_iota(jnp.int32, (sectors, sectors * LANES), 1)
    ones = jnp.where((lane >= row * LANES) & (lane < (row + 1) * LANES), 1.0, 0.0).astype(jnp.bfloat16)
    rest, terms = supply_ref[...], []
    for _ in range(3):
        terms.append(rest.astype(jnp.bfloat16))
        rest = rest - terms[-1].astype(jnp.float32)
    spread_ref[...] = lax.dot_general(
        jnp.concatenate(terms, axis=0), jnp.concatenate([ones] * 3, axis=0), (((0,), (0,)), ((), ())),
        preferred_element_type=jnp.float32,
    )


def prepare(slopes, here, columns, productivity_ref, workers_ref, wage, part_ref, spread_ref, supply_ref):
    sectors, rows = productivity_ref.shape
    pieces = rows // LANES
    supply = supply_of(slopes, productivity_ref, wage)
    for p in range(pieces):
        supply_ref[:, p * LANES:(p + 1) * LANES] = supply[p]
    spread_over_lanes(supply_ref, spread_ref)
    least = functools.reduce(jnp.minimum, supply)
    least = jnp.min(jnp.min(least, axis=0, keepdims=True), axis=1, keepdims=True)
    income = wage * workers_ref[...]
    guarded = jnp.where(least > SMALLEST, income, jnp.nan)
    for i in range(columns // rows):
        part_ref[i * pieces:(i + 1) * pieces, columns:columns + LANES] = guarded * here[i:i + 1]


def send_phi(totals_ref, part_ref, send_ref):
    sectors, _, columns = totals_ref.shape
    for j in range(sectors):
        for k in range(columns // LANES):
            lanes = slice(k * LANES, (k + 1) * LANES)
            part_ref[j:j + 1, lanes] = jnp.sum(totals_ref[j, :, lanes], axis=0, keepdims=True)
    part = part_ref[...]
    for copy in range(send_ref.shape[0]):
        send_ref[copy] = part


def first_phi_kernel(
    cost_in_ref, slope_in_ref, productivity_in_ref, workers_in_ref, wage_in_ref,
    send_ref, spread_ref, trade_ref, facts_ref,
    totals_ref, supply_ref, part_ref, cost_ref, slope_ref, productivity_ref, workers_ref, wage_ref, arrived, brought,
):
    sectors, rows = productivity_ref.shape
    columns = cost_ref.shape[1]
    batch, height = rows // arrived.shape[0], 32
    small = [
        pltpu.make_async_copy(given, held, brought.at[i])
        for i, (given, held) in enumerate(
            ((slope_in_ref, slope_ref), (wage_in_ref, wage_ref), (productivity_in_ref, productivity_ref), (workers_in_ref, workers_ref))
        )
    ]
    copies = []
    for i in range(arrived.shape[0]):
        some = pl.ds(i * batch, batch)
        copies.append(pltpu.make_async_copy(cost_in_ref.at[some], cost_ref.at[some], arrived.at[i]))
    for copy in small + copies:
        copy.start()
    part = lax.axis_index("far") * INNER + lax.axis_index("near") - lax.axis_index("dest") * (columns // rows)
    row = lax.broadcasted_iota(jnp.int32, (sectors, LANES), 0)
    facts_ref[sectors:, :] = jnp.where(row == part, 1.0, 0.0)
    for copy in small:
        copy.wait()
    facts_ref[:sectors, :] = pick(slope_ref, sectors)
    facts = facts_ref[...]
    prepare(facts[:sectors], facts[sectors:], columns, productivity_ref, workers_ref, wage_ref[...], part_ref, spread_ref, supply_ref)
    slopes = [-slope_ref[j] for j in range(sectors)]
    totals_ref[...] = jnp.zeros_like(totals_ref)

    def step(block, carry):
        at = pl.ds(pl.multiple_of(block * height, height), height)
        for k in range(columns // LANES):
            lanes = slice(k * LANES, (k + 1) * LANES)
            cost = cost_ref[at, lanes].astype(jnp.float32)
            for j in range(sectors):
                trade = jnp.exp(cost * slopes[j])
                trade_ref[j, at, lanes] = trade
                term = trade * spread_ref[at, j * LANES:(j + 1) * LANES]
                totals_ref[j, :, lanes] += tree_sum([term[r:r + 8] for r in range(0, height, 8)])
        return carry

    for i, copy in enumerate(copies):
        copy.wait()
        lax.fori_loop(i * batch // height, (i + 1) * batch // height, step, 0, unroll=2)
    send_phi(totals_ref, part_ref, send_ref)


def phi_kernel(gain, facts_ref, trade_ref, productivity_ref, workers_ref, wage_ref, sales_ref, send_ref, spread_ref, new_wage_ref, totals_ref, supply_ref, part_ref):
    sectors, rows, columns = trade_ref.shape
    blocks = columns // LANES
    wage = next_wage(wage_ref, workers_ref, sales_ref, gain)
    new_wage_ref[...] = wage
    prepare(facts_ref[:sectors], facts_ref[sectors:], columns, productivity_ref, workers_ref, wage, part_ref, spread_ref, supply_ref)
    for j in range(sectors):
        def step(block, totals):
            at = pl.ds(pl.multiple_of(block * 8, 8), 8)
            weight = spread_ref[at, j * LANES:(j + 1) * LANES]
            return tuple(totals[k] + trade_ref[j, at, k * LANES:(k + 1) * LANES] * weight for k in range(blocks))

        zero = jnp.zeros((8, LANES), jnp.float32)
        totals = lax.fori_loop(0, rows // 8, step, (zero,) * blocks, unroll=64)
        for k in range(blocks):
            totals_ref[j, :, k * LANES:(k + 1) * LANES] = totals[k]
    send_phi(totals_ref, part_ref, send_ref)


def sum_kernel(got_ref, send_ref):
    total = jnp.sum(got_ref[...], axis=0)
    for copy in range(send_ref.shape[0]):
        send_ref[copy] = total


def sales_kernel(last, facts_ref, trade_ref, spread_ref, preference_ref, got_ref, send_ref, *rest):
    total_ref, ratio_ref, sums_ref = rest[-3:]
    sectors, rows, columns = trade_ref.shape
    blocks = columns // LANES
    sums_ref[...] = jnp.sum(got_ref[...], axis=0)
    preference = preference_ref[...]
    share = preference / jnp.sum(preference, axis=0, keepdims=True)
    for k in range(blocks):
        lanes = slice(k * LANES, (k + 1) * LANES)
        phi = sums_ref[:, lanes]
        ratio = share[:, lanes] * sums_ref[k:k + 1, columns:columns + LANES] / phi
        ratio_ref[:, lanes] = jnp.where(phi < LARGEST, ratio, jnp.nan)
    if last:
        slopes = facts_ref[:sectors]
        for k in range(blocks):
            lanes = slice(k * LANES, (k + 1) * LANES)
            rest[0][:, lanes] = -jnp.log(sums_ref[:, lanes]) / slopes
    for j in range(sectors):
        ratios = [
            jnp.broadcast_to(ratio_ref[j:j + 1, k * LANES:(k + 1) * LANES], (8, LANES))
            for k in range(blocks)
        ]

        def step(block, carry):
            at = pl.ds(pl.multiple_of(block * 8, 8), 8)
            terms = [trade_ref[j, at, k * LANES:(k + 1) * LANES] * ratios[k] for k in range(blocks)]
            total = tree_sum(terms) * spread_ref[at, j * LANES:(j + 1) * LANES]
            total_ref[at, :] = total if j == 0 else total_ref[at, :] + total
            return carry

        lax.fori_loop(0, rows // 8, step, 0, unroll=32)
    for p in range(rows // LANES):
        piece = jnp.sum(jnp.transpose(total_ref[p * LANES:(p + 1) * LANES, :]), axis=0, keepdims=True)
        send_ref[:, p, :] = jnp.broadcast_to(piece, (send_ref.shape[0], LANES))


def settle_kernel(workers_ref, wage_ref, sales_ref, raw_ref, send_ref):
    raw = next_wage(wage_ref, workers_ref, sales_ref)
    raw_ref[...] = raw
    for row, wage in enumerate((raw, wage_ref[...])):
        world = jnp.sum(wage * workers_ref[...], axis=0, keepdims=True)
        send_ref[:, row, :] = jnp.broadcast_to(world, (send_ref.shape[0], LANES))


def finish_kernel(cells, raw_ref, price_ref, got_ref, wage_ref, log_price_ref, world_ref):
    sums = jnp.sum(jnp.sum(got_ref[...], axis=0), axis=1, keepdims=True)
    wage_ref[...] = raw_ref[...] * (cells / sums[0:1])
    log_price_ref[...] = price_ref[...] + jnp.log(cells / sums[1:2])
    world_ref[...] = jnp.broadcast_to(sums[0:1], (1, LANES))


VM = pl.BlockSpec(memory_space=pltpu.VMEM)
SM = pl.BlockSpec(memory_space=pltpu.SMEM)


def call(body, out_shape, scalars, arrays, scratch=(), in_place=()):
    return pl.pallas_call(
        body,
        out_shape=tuple(out_shape),
        in_specs=[SM] * len(scalars) + [VM] * len(arrays) + [pl.BlockSpec(memory_space=pl.ANY)] * len(in_place),
        out_specs=(VM,) * len(out_shape),
        scratch_shapes=[pltpu.VMEM(s, jnp.float32) if isinstance(s, tuple) else s for s in scratch],
        compiler_params=pltpu.CompilerParams(vmem_limit_bytes=16 << 20),
    )(*scalars, *arrays, *in_place)


def exchange(x, axis):
    return lax.all_to_all(x, axis, 0, 0, tiled=True)


def gather(x, axis):
    return exchange(jnp.broadcast_to(x, (lax.axis_size(axis), *x.shape)), axis)


def careful(log_cost, elasticity, productivity, preference, workers, start_wage):
    rows, columns = log_cost.shape
    sectors = elasticity.shape[0]
    across = lax.axis_size(ORIG)
    cells, width = rows * across, columns // across
    spend_share = preference / jnp.sum(preference, axis=0, keepdims=True)

    def settle(raw_wage, wanted):
        world_income = jnp.sum(gather(jnp.sum(raw_wage * workers, keepdims=True), ORIG))
        wage = raw_wage * (cells / world_income)
        if not wanted:
            return wage, None
        incomes = gather(wage * workers, ORIG).reshape(cells)
        return wage, lax.dynamic_slice_in_dim(incomes, lax.axis_index("dest") * columns, columns)

    def kernel_of(slope):
        return jnp.exp(-slope * log_cost.astype(jnp.float32))

    def phi_term(pair):
        return jnp.dot(pair[1], kernel_of(pair[0]), precision=lax.Precision.HIGHEST)

    def sales_term(pair):
        return jnp.dot(kernel_of(pair[0]), pair[1], precision=lax.Precision.HIGHEST)

    def whole(x):
        return jnp.moveaxis(gather(x, ORIG), 0, 1).reshape(sectors, columns)

    wage, dest_income = settle(start_wage, True)
    for step in range(ITERS):
        supply = productivity * jnp.exp(-elasticity[:, None] * jnp.log(wage)[None, :])
        spending = spend_share * dest_income[None, :]
        partial_phi = lax.map(phi_term, (elasticity, supply)).reshape(sectors, across, width)
        phi = whole(jnp.sum(exchange(jnp.moveaxis(partial_phi, 1, 0), ORIG), axis=0))
        log_price = -jnp.log(phi) / elasticity[:, None]
        partial_sales = lax.map(sales_term, (elasticity, spending / phi))
        revenue = jnp.sum(gather(jnp.sum(supply * partial_sales, axis=0), "dest"), axis=0)
        raw_wage = wage * jnp.sqrt(revenue / (wage * workers))
        wage, dest_income = settle(raw_wage, step + 1 < ITERS)
    return wage, log_price


def fast(log_cost, elasticity, productivity, preference, workers, start_wage):
    sectors, rows = productivity.shape
    columns = log_cost.shape[1]
    outer, along = lax.axis_size("far"), lax.axis_size("dest")
    cells = float(rows * outer * INNER)
    pieces, width = rows // LANES, columns + LANES
    workers = workers.reshape(pieces, LANES)
    wage = start_wage.reshape(pieces, LANES)
    sales = trade = None
    for step in range(ITERS):
        last = step + 1 == ITERS
        outs = [f32(outer, sectors, width), f32(rows, sectors * LANES)]
        scratch = [(sectors, 8, columns), (sectors, rows), (sectors, width)]
        if step == 0:
            send, spread, trade, facts = call(
                first_phi_kernel, outs + [f32(sectors, rows, columns), f32(2 * sectors, LANES)], [], [],
                scratch + [pltpu.VMEM(log_cost.shape, log_cost.dtype), pltpu.SMEM((sectors,), jnp.float32)]
                + [(sectors, rows), (pieces, LANES), (pieces, LANES)]
                + [pltpu.SemaphoreType.DMA((2,)), pltpu.SemaphoreType.DMA((4,))],
                [log_cost, elasticity, productivity, workers, wage],
            )
        else:
            send, spread, wage = call(
                functools.partial(phi_kernel, GAINS[step - 1]),
                outs + [f32(pieces, LANES)], [],
                [facts, trade, productivity, workers, wage, sales], scratch,
            )
        got = exchange(send, "far")
        send, = call(sum_kernel, [f32(INNER, sectors, width)], [], [got])
        got = exchange(send, "near")
        made = call(
            functools.partial(sales_kernel, last),
            [f32(along, pieces, LANES)] + ([f32(sectors, columns)] if last else []),
            [],
            [facts, trade, spread, preference, got],
            [(rows, LANES), (sectors, columns), (sectors, width)],
        )
        sales = exchange(made[0], "dest")
    raw, send = call(settle_kernel, [f32(pieces, LANES), f32(outer * INNER, 2, LANES)], [], [workers, wage, sales])
    got = exchange(send, ORIG)
    wage, log_price, world = call(
        functools.partial(finish_kernel, cells),
        [f32(pieces, LANES), f32(sectors, columns), f32(1, LANES)], [], [raw, made[1], got],
    )
    return wage.reshape(rows), log_price, world[0, 0]


def on_device(*args):
    wage, log_price, world = fast(*args)
    done = lax.while_loop(
        lambda state: ~state[2],
        lambda state: (*careful(*args), jnp.bool_(True)),
        (wage, log_price, jnp.isfinite(world)),
    )
    return done[:2]


def solution(mesh):
    across, along = mesh.devices.shape
    split = Mesh(mesh.devices.reshape(across // INNER, INNER, along), (*ORIG, "dest"))
    return jax.shard_map(
        on_device,
        mesh=split,
        in_specs=(P(ORIG, "dest"), P(), P(None, ORIG), P(None, "dest"), P(ORIG), P(ORIG)),
        out_specs=(P(ORIG), P(None, "dest")),
        check_vma=False,
    )
```
